128 devices in a mesh: gx: 16 (over z_hi, x, core), gy: 8 (over y, z_lo).
Axes of the slice: x: 4, y: 4, z: 4 (z_hi: 2, z_lo: 2; z = z_hi * 2 + z_lo), core: 2. Of those that a mesh axis runs over, the one named last changes fastest.
Arguments:
- checkpoint: float32 [8, 64, 65536], P('gy', 'gx'), may hold values from 0.2 to 2
- sorption_kd: float32 [512, 65536], P('gy', 'gx'), may hold values from 0.05 to 1
- velocity: float32 [3, 512, 65536], P(None, 'gy', 'gx'), may hold values from -0.5 to 0.5
- source: float32 [512, 65536], P('gy', 'gx'), may hold values from -8 to 8
- target: float32 [512, 65536], P('gy', 'gx'), may hold values from -6 to 6
- cell_type: int32 [512, 65536], P('gy', 'gx'), may hold values from 0 to 2
- outlets: int32 [1024], replicated, may hold values from 0 to 33554431, as said below
Outputs:
- kd_gradient: float32 [512, 65536], P('gy', 'gx')
- checkpoint_adjoint: float32 [512, 65536], P('gy', 'gx')
The draws below stay inside these ranges and needn't reach their ends.
Inputs may be any that keep to these rules, and one draw needn't show every extreme that they name: `outlets`: 1024 distinct cells.
All inputs are finite; a program needn't handle non-finite values.
Results may differ from the reference program's by a relative error of at most 0.00002.
Values sent between devices are 32-bit elements; how exact they have to be, the bound alone decides.
No kernel may reach another device: no remote copies, remote signals or barrier semaphores. Data moves between devices by JAX's collectives and lax.ppermute only.
A program may use at most 192 MiB of HBM per device.

```python
import math
import jax
import jax.numpy as jnp

BY = 64
NZ = 64
NOUT = 1024
NX = 1024
NY = 512
N_GY = 8


def draw_outlets(key, part):
    key = jax.random.fold_in(key, 5)
    band = NY * NX * NZ // NOUT
    offset = jax.random.randint(key, (NOUT,), 0, band)
    return (jnp.arange(NOUT, dtype=jnp.int32) * band + offset).astype(jnp.int32)


def touch_ends(entries, key, low, largest):
    dims = entries.shape
    place = [jax.random.randint(jax.random.fold_in(key, axis), (), 0, dims[axis]) for axis in range(len(dims))]
    entries = entries.at[tuple(place)].set(low)
    longest = dims.index(max(dims))
    place[longest] = (place[longest] + 1) % dims[longest]
    return entries.at[tuple(place)].set(largest)


def levels(stream_key, dims, pieces, smallest, top_value):
    factor_of = 1.0
    for dim, shards_of in pieces:
        steps = jax.random.uniform(jax.random.fold_in(jax.random.fold_in(stream_key, 6), dim), (shards_of,), jnp.float32, smallest / len(pieces), top_value / len(pieces))
        factor_of = factor_of * jnp.repeat(jnp.exp(steps), dims[dim] // shards_of).reshape((-1,) + (1,) * (len(dims) - 1 - dim))
    return factor_of


def bell_draw(own_key, shape, width, bound, cuts=(), kind=jnp.bfloat16):
    entries = jax.random.normal(own_key, shape, jnp.float32) * width
    if len(cuts) > 0:
        entries = levels(own_key, shape, cuts, -0.22, 0.18) * entries
    return jnp.clip(entries, min=-bound, max=bound).astype(kind)


def setup_inputs(seed: int = 0) -> dict:
    streams_of = jax.random.split(jax.random.key(seed), 8)
    return {
        "checkpoint": jnp.clip(jnp.exp(math.log(2.0) - 2.3025851 * jax.random.uniform(streams_of[0], (N_GY, BY, NX * NZ), jnp.float32) ** levels(streams_of[0], (N_GY, BY, NX * NZ), ((0, 8), (1, 16)), -0.2, 0.2)), 0.2, 2.0),
        "sorption_kd": jnp.clip(jnp.exp(math.log(1.0) - 2.9957323 * jax.random.uniform(streams_of[1], (NY, NX * NZ), jnp.float32) ** levels(streams_of[1], (NY, NX * NZ), ((0, 8), (1, 16)), -0.2, 0.2)), 0.05, 1.0),
        "velocity": jnp.clip(jax.random.uniform(streams_of[2], (3, NY, NX * NZ), jnp.float32, -0.5, 0.5) * levels(streams_of[2], (3, NY, NX * NZ), ((1, 8), (2, 16)), -0.4, 0.0), -0.5, 0.5),
        "source": bell_draw(streams_of[3], (NY, NX * NZ), 2.0, 8.0, ((0, 8), (1, 16)), jnp.float32),
        "target": bell_draw(streams_of[4], (NY, NX * NZ), 1.0, 6.0, ((0, 8), (1, 16)), jnp.float32),
        "cell_type": touch_ends(jax.random.randint(streams_of[5], (NY, NX * NZ), 0, 3), jax.random.fold_in(streams_of[5], 1), 0, 2).astype(jnp.int32),
        "outlets": draw_outlets(jax.random.fold_in(streams_of[7], 71), 0),
    }


BULK = 4.0
FREUND = 0.7
DISP = 0.1
DRAIN = 0.5
STEP = 0.4
OUTLET_W = 4.0

def vertical_terms(tracer, vel_z):
    upper_cell = jnp.concatenate([tracer[..., 1:], tracer[..., -1:]], axis=-1)
    lower_cell = jnp.concatenate([tracer[..., :1], tracer[..., :-1]], axis=-1)
    return DISP * (upper_cell + lower_cell - 2.0 * tracer) - jnp.maximum(vel_z, 0.0) * (tracer - lower_cell) - jnp.minimum(vel_z, 0.0) * (upper_cell - tracer)

def total_flux(tracer, padded, velocity, cell_type, source):
    north_cell = padded[2:, 1:-1]
    south_cell = padded[:-2, 1:-1]
    east_cell = padded[1:-1, 2:]
    west_cell = padded[1:-1, :-2]
    plane = DISP * (north_cell + south_cell + east_cell + west_cell - 4.0 * tracer)
    plane = plane - jnp.maximum(velocity[0], 0.0) * (tracer - south_cell) - jnp.minimum(velocity[0], 0.0) * (north_cell - tracer)
    plane = plane - jnp.maximum(velocity[1], 0.0) * (tracer - west_cell) - jnp.minimum(velocity[1], 0.0) * (east_cell - tracer)
    drains = (cell_type == 2).astype(jnp.float32)
    wells = (cell_type == 1).astype(jnp.float32)
    return plane + vertical_terms(tracer, velocity[2]) - DRAIN * drains * tracer + wells * source

def reference(checkpoint, sorption_kd, velocity, source, target, cell_type, outlets):
    shape3 = (NY, NX, NZ)
    initial = checkpoint.reshape(shape3)
    kd_field = sorption_kd.reshape(shape3)
    flow = velocity.reshape((3,) + shape3)
    source_field = source.reshape(shape3)
    kinds = cell_type.reshape(shape3)
    target_field = target.reshape(shape3)

    def forward(start_state, sorption):
        retard = 1.0 + BULK * sorption * start_state ** (FREUND - 1.0)
        tracer = start_state
        for repeat in range(2):
            padded = jnp.pad(tracer, ((1, 1), (1, 1), (0, 0)))
            tracer = tracer + STEP * total_flux(tracer, padded, flow, kinds, source_field) / retard
        return tracer
    final_state, pullback = jax.vjp(forward, initial, kd_field)
    weight = jnp.ones((NY * NX * NZ,), jnp.float32).at[outlets].add(OUTLET_W).reshape(shape3)
    misfit = weight * (final_state - target_field)
    grad_start, grad_kd = pullback(misfit)
    return (grad_kd.reshape(NY, NX * NZ), grad_start.reshape(NY, NX * NZ))
```

```python
import jax
import jax.numpy as jnp
from jax import lax
from jax.experimental import pallas as pl
from jax.experimental.pallas import tpu as pltpu
from jax.sharding import PartitionSpec as P

NZ = 64
BULK = 4.0
FREUND = 0.7
DISP = 0.1
DRAIN = 0.5
STEP = 0.4
OUTLET_W = 4.0

LANES = 128
ROWS = 64
TILES = 32
WT = TILES + 4
WR = 80
BASE = 8
COLS = TILES * LANES
WCOLS = WT * LANES
MCOLS = WCOLS + 4 * LANES
F32 = jnp.float32
MIB = 1 << 20

VM = pl.BlockSpec(memory_space=pltpu.VMEM)
SM = pl.BlockSpec(memory_space=pltpu.SMEM)
HB = pl.BlockSpec(memory_space=pl.ANY)


def window(dtype=F32):
    return jax.ShapeDtypeStruct((WT, WR, LANES), dtype)


def lane_iota(rows):
    return lax.broadcasted_iota(jnp.int32, (rows, LANES), 1)


def pack_lines(src, out, sem):
    n = out.shape[0]
    copies = []
    for i in range(n):
        low = i * COLS - 2 * LANES
        high = low + WCOLS
        pieces = [(max(low, 0), min(high, n * COLS), max(-low, 0))]
        if low < 0:
            pieces.append((0, 2 * LANES, 0))
        if high > n * COLS:
            pieces.append((n * COLS - 2 * LANES, n * COLS, WCOLS - 2 * LANES))
        for a, b, at in pieces:
            copies.append(
                pltpu.make_async_copy(
                    src.at[0, :, a:b], out.at[i, :, at : at + b - a], sem
                )
            )
    for c in copies:
        c.start()
    for c in copies:
        c.wait()


def pack_edges(kdl, kdr, kdt, kdb, vl, vr, vt, vb, sl, sr, st, sb, cl, cr, ct, cb, tl, tr, tt, tb,
               to_left, to_right, to_low, to_high):
    lo = lane_iota(ROWS) < NZ

    def seven(kd, v, s, c, t, at):
        kind = at(c)
        return (
            at(kd), at(v, 0), at(v, 1), at(v, 2),
            jnp.where(kind == 1, at(s), 0.0),
            jnp.where(kind == 2, DRAIN, 0.0).astype(F32),
            at(t),
        )

    def cols(tile):
        def at(ref, d=None):
            part = pl.ds(tile * LANES, LANES)
            return ref[:, part] if d is None else ref[d, :, part]
        return at

    full = seven(kdl, vl, sl, cl, tl, cols(0))
    third = seven(kdl, vl, sl, cl, tl, cols(1))
    for f in range(7):
        to_left[f] = full[f]
    for p in range(3):
        to_left[7 + p] = jnp.where(lo, third[2 * p], pltpu.roll(third[2 * p + 1], NZ, 1))
    full = seven(kdr, vr, sr, cr, tr, cols(1))
    third = seven(kdr, vr, sr, cr, tr, cols(0))
    for f in range(7):
        to_right[f] = full[f]
    for p in range(3):
        to_right[7 + p] = jnp.where(lo, pltpu.roll(third[2 * p], NZ, 1), third[2 * p + 1])

    def rows(a):
        def at(ref, d=None):
            return ref[a : a + 2, :] if d is None else ref[d, a : a + 2, :]
        return at

    for f, part in enumerate(seven(kdt, vt, st, ct, tt, rows(0))):
        to_low[f] = part
    for f, part in enumerate(seven(kdb, vb, sb, cb, tb, rows(6))):
        to_high[f] = part


def list_outlets(outlets, place, found, count):
    row_start, col_start = place[0], place[1]

    def step(i, n):
        for k in range(8):
            flat = outlets[i * 8 + k]
            row = (flat >> 16) - row_start + BASE
            col = ((flat >> 6) & 1023) - col_start + 4
            inside = (row >= BASE - 2) & (row < BASE + ROWS + 2) & (col >= 2) & (col < 70)
            found[n] = (row << 16) + (col << 6) + (flat & 63)
            n = n + inside.astype(jnp.int32)
        return n

    count[0] = lax.fori_loop(0, outlets.shape[0] // 8, step, jnp.int32(0))


def coefficients(v0, v1, v2, drain):
    z = lax.broadcasted_iota(jnp.int32, v0.shape, v0.ndim - 1) & (NZ - 1)
    north = DISP - jnp.minimum(v0, 0.0)
    south = DISP + jnp.maximum(v0, 0.0)
    east = DISP - jnp.minimum(v1, 0.0)
    west = DISP + jnp.maximum(v1, 0.0)
    up = jnp.where(z == NZ - 1, 0.0, DISP - jnp.minimum(v2, 0.0))
    down = jnp.where(z == 0, 0.0, DISP + jnp.maximum(v2, 0.0))
    centre = ((north + south) + (east + west)) + ((up + down) + drain)
    return north, south, east, west, up, down, centre


def flux(u, coef, src, t, left, right, a, rows):
    cn, cs, ce, cw, cu, cd, cc = coef
    here = pl.ds(a, rows)
    lo = lane_iota(rows) < NZ
    mid = u[t, here, :]
    north = u[t, pl.ds(a + 1, rows), :]
    south = u[t, pl.ds(a - 1, rows), :]
    east = pltpu.roll(jnp.where(lo, u[right, here, :], mid), NZ, 1)
    west = pltpu.roll(jnp.where(lo, mid, u[left, here, :]), NZ, 1)
    upper = pltpu.roll(mid, LANES - 1, 1)
    lower = pltpu.roll(mid, 1, 1)
    plane = cn[t, here, :] * north + cs[t, here, :] * south
    plane = plane + (ce[t, here, :] * east + cw[t, here, :] * west)
    plane = plane + (cu[t, here, :] * upper + cd[t, here, :] * lower)
    return mid, plane + (src[t, here, :] - cc[t, here, :] * mid)


def flux_back(w, coef, t, left, right, a, rows):
    cn, cs, ce, cw, cu, cd, cc = coef
    here = pl.ds(a, rows)
    above, below = pl.ds(a + 1, rows), pl.ds(a - 1, rows)
    lo = lane_iota(rows) < NZ
    mid = w[t, here, :]
    w_right, w_left = w[right, here, :], w[left, here, :]
    from_low = cw[right, here, :] * w_right + ce[t, here, :] * mid
    from_high = cw[t, here, :] * mid + ce[left, here, :] * w_left
    total = pltpu.roll(jnp.where(lo, from_low, from_high), NZ, 1)
    total = total + (cs[t, above, :] * w[t, above, :] + cn[t, below, :] * w[t, below, :])
    total = total + pltpu.roll(cd[t, here, :] * mid, LANES - 1, 1)
    total = total + pltpu.roll(cu[t, here, :] * mid, 1, 1)
    return total - cc[t, here, :] * mid


def sorb(u):
    return jnp.exp((FREUND - 1.0) * jnp.log(u))


def rate_of(kd, power):
    return STEP / (1.0 + BULK * kd * power)


def first_half(place, lines, xl, xr, kd_h, v_h, s_h, c_h,
               u0, fst, d1, rate, power, cn, cs, ce, cw, cu, cd, cc, src, up_msg, low_msg,
               kd, v, s, c, sems):
    loads = [
        pltpu.make_async_copy(a, b, sems.at[k])
        for k, (a, b) in enumerate(((kd_h, kd), (v_h, v), (s_h, s), (c_h, c)))
    ]
    for load in loads:
        load.start()
    coef = (cn, cs, ce, cw, cu, cd, cc)
    own = pl.ds(BASE, ROWS)
    lines_of = lines.shape[1]
    for k in range(lines.shape[0]):
        for t in range(WT):
            u0[t, BASE + lines_of * k : BASE + lines_of * (k + 1), :] = lines[
                k, :, t * LANES : (t + 1) * LANES
            ]
    lo = lane_iota(ROWS) < NZ

    def third(ref, f, high):
        both = ref[7 + f // 2]
        if high:
            return jnp.where(lo, 0.0, both if f % 2 else pltpu.roll(both, NZ, 1))
        return jnp.where(lo, pltpu.roll(both, NZ, 1) if f % 2 else both, 0.0)

    for tile, fields in (
        (0, [third(xl, f, True) for f in range(6)]),
        (1, [xl[f] for f in range(6)]),
        (WT - 2, [xr[f] for f in range(6)]),
        (WT - 1, [third(xr, f, False) for f in range(6)]),
    ):
        for ref, val in zip(coef, coefficients(*fields[1:4], fields[5])):
            ref[tile, own, :] = val
        src[tile, own, :] = fields[4]
        rate[tile, own, :] = rate_of(fields[0], sorb(u0[tile, own, :]))

    @pl.when(place[0] == 0)
    def _():
        for ref in (u0, rate):
            ref[0:2, own, :] = jnp.zeros((2, ROWS, LANES), F32)

    @pl.when(place[1] == 0)
    def _():
        for ref in (u0, rate):
            ref[WT - 2 : WT, own, :] = jnp.zeros((2, ROWS, LANES), F32)

    loads[0].wait()

    def rates(t, carry):
        for r in range(0, ROWS, 8):
            at = pl.ds(BASE + r, 8)
            p = sorb(u0[t + 2, at, :])
            power[t, pl.ds(r, 8), :] = p
            rate[t + 2, at, :] = rate_of(kd[pl.ds(r, 8), pl.ds(pl.multiple_of(t * LANES, LANES), LANES)], p)
        return carry

    lax.fori_loop(0, TILES, rates, 0)
    for load in loads[1:]:
        load.wait()

    def coefs(t, carry):
        at = pl.ds(pl.multiple_of(t * LANES, LANES), LANES)
        for r in range(0, ROWS, 8):
            rr, to = pl.ds(r, 8), pl.ds(BASE + r, 8)
            kind = c[rr, at]
            drain = jnp.where(kind == 2, DRAIN, 0.0).astype(F32)
            for ref, val in zip(coef, coefficients(v[0, rr, at], v[1, rr, at], v[2, rr, at], drain)):
                ref[t + 2, to, :] = val
            src[t + 2, to, :] = jnp.where(kind == 1, s[rr, at], 0.0)
        return carry

    lax.fori_loop(0, TILES, coefs, 0)

    def step(t, carry):
        left, right = jnp.maximum(t - 1, 0), jnp.minimum(t + 1, WT - 1)
        for r in range(BASE, BASE + ROWS, 8):
            at = pl.ds(r, 8)
            mid, f = flux(u0, coef, src, t, left, right, r, 8)
            d = rate[t, at, :] * f
            d1[t, at, :] = d
            fst[t, at, :] = mid + d
        return carry

    lax.fori_loop(0, WT, step, 0)

    top = BASE + ROWS
    for t in range(WT):
        at = pl.ds(t * LANES, LANES)
        up_msg[0:2, at] = u0[t, top - 2 : top, :]
        up_msg[2:4, at] = fst[t, top - 3 : top - 1, :]
        low_msg[0:2, at] = u0[t, BASE : BASE + 2, :]
        low_msg[2:4, at] = fst[t, BASE + 1 : BASE + 3, :]
    for k in range(16):
        at = pl.ds(WCOLS + (k % 4) * LANES, LANES)
        row = pl.ds(k // 4, 1)
        if k < 14:
            side = xr if k % 2 else xl
            up_msg[row, at] = side[k // 2, ROWS - 1 : ROWS, :]
            low_msg[row, at] = side[k // 2, 0:1, :]
        else:
            up_msg[row, at] = jnp.zeros((1, LANES), F32)
            low_msg[row, at] = jnp.zeros((1, LANES), F32)


def second_half(place, found, count, xl, xr, yl, yh, ml, mh, kd_h, t_h, power,
                u0_in, fst_in, d1_in, rate_in, cn_in, cs_in, ce_in, cw_in, cu_in, cd_in, cc_in, src_in,
                kd_out, start_out,
                u0, fst, d1, rate, cn, cs, ce, cw, cu, cd, cc, src,
                kd, tgt, halo, target, d2, mis, w, grad, w1, sems):
    loads = [
        pltpu.make_async_copy(a, b, sems.at[k]) for k, (a, b) in enumerate(((kd_h, kd), (t_h, tgt)))
    ]
    for load in loads:
        load.start()
    coef = (cn, cs, ce, cw, cu, cd, cc)
    low8, high8 = slice(0, BASE), slice(BASE + ROWS, WR)
    own = pl.ds(BASE, ROWS)

    halo[...] = jnp.zeros(halo.shape, F32)
    top = BASE + ROWS
    for f in range(7):
        for t in range(TILES):
            at = pl.ds(t * LANES, LANES)
            halo[f, t + 2, 6:8, :] = yl[f, :, at]
            halo[f, t + 2, 8:10, :] = yh[f, :, at]
        for side, tile in ((0, 1), (1, WT - 2)):
            k = 2 * f + side
            at = pl.ds(WCOLS + (k % 4) * LANES, LANES)
            row = pl.ds(k // 4, 1)
            halo[f, tile, 7:8, :] = ml[row, at]
            halo[f, tile, 8:9, :] = mh[row, at]
    for t in range(WT):
        at = pl.ds(t * LANES, LANES)
        u0[t, low8, :] = jnp.ones((BASE, LANES), F32)
        u0[t, high8, :] = jnp.ones((BASE, LANES), F32)
        fst[t, low8, :] = jnp.zeros((BASE, LANES), F32)
        fst[t, high8, :] = jnp.zeros((BASE, LANES), F32)
        u0[t, 6:8, :] = ml[0:2, at]
        fst[t, 5:7, :] = ml[2:4, at]
        u0[t, top : top + 2, :] = mh[0:2, at]
        fst[t, top + 1 : top + 3, :] = mh[2:4, at]

    def edges(t, carry):
        for a, to in ((0, low8), (8, high8)):
            at = pl.ds(a, 8)
            values = coefficients(halo[1, t, at, :], halo[2, t, at, :], halo[3, t, at, :], halo[5, t, at, :])
            for ref, val in zip(coef, values):
                ref[t, to, :] = val
            src[t, to, :] = halo[4, t, at, :]
            rate[t, to, :] = rate_of(halo[0, t, at, :], sorb(u0[t, to, :]))
            target[t, to, :] = halo[6, t, at, :]
        return carry

    lax.fori_loop(0, WT, edges, 0)

    zero8 = jnp.zeros((WT, BASE, LANES), F32)

    @pl.when(place[0] == 0)
    def _():
        rate[0:2] = jnp.zeros((2, WR, LANES), F32)
        u0[0:2] = jnp.zeros((2, WR, LANES), F32)

    @pl.when(place[1] == 0)
    def _():
        rate[WT - 2 : WT] = jnp.zeros((2, WR, LANES), F32)
        u0[WT - 2 : WT] = jnp.zeros((2, WR, LANES), F32)

    @pl.when(place[2] == 0)
    def _():
        rate[:, low8, :] = zero8
        u0[:, low8, :] = zero8
        fst[:, low8, :] = zero8

    @pl.when(place[3] == 0)
    def _():
        rate[:, high8, :] = zero8
        u0[:, high8, :] = zero8
        fst[:, high8, :] = zero8

    def sides(t):
        return jnp.maximum(t - 1, 0), jnp.minimum(t + 1, WT - 1)

    def edge_step(t, carry):
        left, right = sides(t)
        for a, r0 in ((BASE - 4, BASE - 1), (top - 4, top - 1)):
            at = pl.ds(a, 8)
            row = lax.broadcasted_iota(jnp.int32, (8, LANES), 0) + a
            new = (row == r0) | (row == r0 + 1)
            mid, f = flux(u0, coef, src, t, left, right, a, 8)
            d = rate[t, at, :] * f
            d1[t, at, :] = jnp.where(new, d, d1[t, at, :])
            fst[t, at, :] = jnp.where(new, mid + d, fst[t, at, :])
        return carry

    lax.fori_loop(0, WT, edge_step, 0)

    loads[1].wait()

    def targets(t, carry):
        at = pl.ds(pl.multiple_of(t * LANES, LANES), LANES)
        target[t + 2, own, :] = tgt[:, at]
        return carry

    lax.fori_loop(0, TILES, targets, 0)
    target[1, own, :] = xl[6]
    target[WT - 2, own, :] = xr[6]

    spans = range(BASE - 4, BASE + ROWS + 4, 8)

    def step(t, carry):
        for a in spans:
            at = pl.ds(a, 8)
            mid, f = flux(fst, coef, src, t, t - 1, t + 1, a, 8)
            rt = rate[t, at, :]
            d = rt * f
            d2[t, at, :] = d
            m = (mid + d) - target[t, at, :]
            mis[t, at, :] = m
            w[t, at, :] = m * rt
        return carry

    lax.fori_loop(1, WT - 1, step, 0)
    for tile in (0, WT - 1):
        w[tile] = jnp.zeros((WR, LANES), F32)
        w1[tile] = jnp.zeros((WR, LANES), F32)

    lane = lax.broadcasted_iota(jnp.int32, (1, LANES), 1)

    def weigh(i, carry):
        code = found[i]
        row, col = code >> 16, (code >> 6) & 127
        hit = lane == (col & 1) * NZ + (code & (NZ - 1))
        tile = col >> 1
        at = pl.ds(row, 1)
        factor = jnp.where(hit, 1.0 + OUTLET_W, 1.0)
        mis[tile, at, :] = mis[tile, at, :] * factor
        w[tile, at, :] = w[tile, at, :] * factor
        return carry

    lax.fori_loop(0, count[0], weigh, 0)

    def back(t, carry):
        for a in spans:
            at = pl.ds(a, 8)
            g = mis[t, at, :] + flux_back(w, coef, t, t - 1, t + 1, a, 8)
            grad[t, at, :] = g
            w1[t, at, :] = g * rate[t, at, :]
        return carry

    lax.fori_loop(1, WT - 1, back, 0)
    loads[0].wait()

    def last(t, carry):
        cols = pl.ds(pl.multiple_of(t * LANES, LANES), LANES)
        tw = t + 2
        for r in range(0, ROWS, 8):
            a = BASE + r
            at, rr = pl.ds(a, 8), pl.ds(r, 8)
            g = grad[tw, at, :]
            start = g + flux_back(w1, coef, tw, tw - 1, tw + 1, a, 8)
            both = mis[tw, at, :] * d2[tw, at, :] + g * d1[tw, at, :]
            kdg = (both * rate[tw, at, :]) * (power[t, rr, :] * (-BULK / STEP))
            kd_out[rr, cols] = kdg
            start_out[rr, cols] = start + kdg * kd[rr, cols] * (FREUND - 1.0) / u0[tw, at, :]
        return carry

    lax.fori_loop(0, TILES, last, 0)


def params(mib):
    return pltpu.CompilerParams(vmem_limit_bytes=mib * MIB)


def shifts(axis):
    n = lax.axis_size(axis)
    up = [(i, i + 1) for i in range(n - 1)]
    return up, [(b, a) for a, b in up]


def per_device(checkpoint, sorption_kd, velocity, source, target, cell_type, outlets):
    n_gx = lax.axis_size("gx")
    gx, gy = lax.axis_index("gx"), lax.axis_index("gy")
    lines = pl.pallas_call(
        pack_lines,
        out_shape=jax.ShapeDtypeStruct((n_gx, checkpoint.shape[1], WCOLS), F32),
        in_specs=[HB],
        out_specs=HB,
        scratch_shapes=[pltpu.SemaphoreType.DMA],
        name="pack_lines",
    )(checkpoint)
    arrived = lax.all_to_all(lines, "gx", split_axis=0, concat_axis=0, tiled=True)

    def edge_specs(lead):
        def spec(shape, index):
            if lead:
                return pl.BlockSpec((lead,) + shape, lambda i: (0,) + index)
            return pl.BlockSpec(shape, lambda i: index)
        return [
            spec((ROWS, 2 * LANES), (0, 0)),
            spec((ROWS, 2 * LANES), (0, TILES // 2 - 1)),
            spec((8, COLS), (0, 0)),
            spec((8, COLS), (ROWS // 8 - 1, 0)),
        ]

    side = jax.ShapeDtypeStruct((10, ROWS, LANES), F32)
    line = jax.ShapeDtypeStruct((7, 2, COLS), F32)
    fields = (sorption_kd, velocity, source, cell_type, target)
    whole = lambda s: pl.BlockSpec(s, lambda i: (0,) * len(s))
    to_left, to_right, to_low, to_high = pl.pallas_call(
        pack_edges,
        grid=(1,),
        out_shape=[side, side, line, line],
        in_specs=[s for f in fields for s in edge_specs(3 if f.ndim == 3 else 0)],
        out_specs=[whole(side.shape)] * 2 + [whole(line.shape)] * 2,
        name="pack_edges",
    )(*[f for f in fields for _ in range(4)])
    x_up, x_down = shifts("gx")
    y_up, y_down = shifts("gy")
    xl = lax.ppermute(to_right, "gx", x_up)
    xr = lax.ppermute(to_left, "gx", x_down)
    yl = lax.ppermute(to_high, "gy", y_up)
    yh = lax.ppermute(to_low, "gy", y_down)

    where = jnp.stack([gy * ROWS, gx * (COLS // NZ)]).astype(jnp.int32)
    found, count = pl.pallas_call(
        list_outlets,
        out_shape=[
            jax.ShapeDtypeStruct((outlets.shape[0],), jnp.int32),
            jax.ShapeDtypeStruct((1,), jnp.int32),
        ],
        in_specs=[SM, SM],
        out_specs=[SM, SM],
        name="list_outlets",
    )(outlets, where)

    edge = jnp.stack([gx, n_gx - 1 - gx, gy, lax.axis_size("gy") - 1 - gy]).astype(jnp.int32)
    message = jax.ShapeDtypeStruct((4, MCOLS), F32)
    power = jax.ShapeDtypeStruct((TILES, ROWS, LANES), F32)
    u0, fst, d1, rate, power, *rest = pl.pallas_call(
        first_half,
        out_shape=[window()] * 4 + [power] + [window()] * 8 + [message] * 2,
        in_specs=[SM] + [VM] * 3 + [HB] * 4,
        out_specs=[VM] * 15,
        scratch_shapes=[
            pltpu.VMEM((ROWS, COLS), F32),
            pltpu.VMEM((3, ROWS, COLS), F32),
            pltpu.VMEM((ROWS, COLS), F32),
            pltpu.VMEM((ROWS, COLS), jnp.int32),
            pltpu.SemaphoreType.DMA((4,)),
        ],
        compiler_params=params(24),
        name="first_half",
    )(edge, arrived, xl, xr, sorption_kd, velocity, source, cell_type)
    coefs, (up_msg, low_msg) = rest[:8], rest[8:]
    ml = lax.ppermute(up_msg, "gy", y_up)
    mh = lax.ppermute(low_msg, "gy", y_down)

    kept = (u0, fst, d1, rate, *coefs)
    plane = jax.ShapeDtypeStruct((ROWS, COLS), F32)
    work = pltpu.VMEM((WT, WR, LANES), F32)
    outs = pl.pallas_call(
        second_half,
        out_shape=[plane, plane] + [window()] * 12,
        in_specs=[SM] * 3 + [VM] * 6 + [HB] * 2 + [VM] * 13,
        out_specs=[VM] * 14,
        input_output_aliases={12 + k: 2 + k for k in range(12)},
        scratch_shapes=[
            pltpu.VMEM((ROWS, COLS), F32),
            pltpu.VMEM((ROWS, COLS), F32),
            pltpu.VMEM((7, WT, 16, LANES), F32),
            work, work, work, work, work, work,
            pltpu.SemaphoreType.DMA((2,)),
        ],
        compiler_params=params(24),
        name="second_half",
    )(edge, found, count, xl, xr, yl, yh, ml, mh, sorption_kd, target, power, *kept)
    return outs[0], outs[1]


def solution(mesh):
    return jax.shard_map(
        per_device,
        mesh=mesh,
        in_specs=(
            P("gy", "gx", None),
            P("gy", "gx"),
            P(None, "gy", "gx"),
            P("gy", "gx"),
            P("gy", "gx"),
            P("gy", "gx"),
            P(),
        ),
        out_specs=(P("gy", "gx"), P("gy", "gx")),
        check_vma=False,
    )
```

```python
import jax
import jax.numpy as jnp
from jax import lax
from jax.experimental import pallas as pl
from jax.experimental.pallas import tpu as pltpu
from jax.sharding import PartitionSpec as P

NZ = 64
BULK = 4.0
FREUND = 0.7
DISP = 0.1
DRAIN = 0.5
STEP = 0.4
OUTLET_W = 4.0

LANES = 128
ROWS = 64
TILES = 32
WT = TILES + 4
WR = 80
BASE = 8
COLS = TILES * LANES
WCOLS = WT * LANES
MCOLS = WCOLS + 4 * LANES
F32 = jnp.float32
MIB = 1 << 20
FIRST_MIB = 30
UNROLL = 2

VM = pl.BlockSpec(memory_space=pltpu.VMEM)
SM = pl.BlockSpec(memory_space=pltpu.SMEM)
HB = pl.BlockSpec(memory_space=pltpu.HBM)


def window(dtype=F32):
    return jax.ShapeDtypeStruct((WT, WR, LANES), dtype)


def lane_iota(rows):
    return lax.broadcasted_iota(jnp.int32, (rows, LANES), 1)


def pack_lines(src, out, sem):
    n = out.shape[0]
    copies = []
    for i in range(n):
        low = i * COLS - 2 * LANES
        high = low + WCOLS
        pieces = [(max(low, 0), min(high, n * COLS), max(-low, 0))]
        if low < 0:
            pieces.append((0, 2 * LANES, 0))
        if high > n * COLS:
            pieces.append((n * COLS - 2 * LANES, n * COLS, WCOLS - 2 * LANES))
        for a, b, at in pieces:
            copies.append(
                pltpu.make_async_copy(
                    src.at[0, :, a:b], out.at[i, :, at : at + b - a], sem
                )
            )
    for c in copies:
        c.start()
    for c in copies:
        c.wait()


def pack_fields(kd, v, s, c, t, stack, to_left, to_right, to_low, to_high):
    step, last = pl.program_id(0), pl.num_programs(0) - 1
    kind = c[...]
    fields = (
        kd[...], v[0], v[1], v[2],
        jnp.where(kind == 1, s[...], 0.0),
        jnp.where(kind == 2, DRAIN, 0.0).astype(F32),
    )
    for f, val in enumerate(fields):
        stack[f] = val
    for f, val in enumerate(fields + (t[...],)):
        to_low[f] = val[0:2]
        to_high[f] = val[ROWS - 2 : ROWS]
    lo = lane_iota(ROWS) < NZ

    def layers(out, near, far, low_side):
        for f in range(6):
            out[f] = stack[f, :, near]
        out[6] = t[:, near]
        for p in range(3):
            first, second = stack[2 * p, :, far], stack[2 * p + 1, :, far]
            if low_side:
                second = pltpu.roll(second, NZ, 1)
            else:
                first = pltpu.roll(first, NZ, 1)
            out[7 + p] = jnp.where(lo, first, second)

    width = kd.shape[1]

    @pl.when(step == 0)
    def _():
        layers(to_left, slice(0, LANES), slice(LANES, 2 * LANES), True)

    @pl.when(step == last)
    def _():
        layers(to_right, slice(width - LANES, width), slice(width - 2 * LANES, width - LANES), False)


def list_outlets(codes, found, count):
    unroll = 32

    def step(i, n):
        values = [codes[i * unroll + k] for k in range(unroll)]
        for value in values:
            found[n] = value
            n = n + 1 + (value >> 31)
        return n

    count[0] = lax.fori_loop(0, codes.shape[0] // unroll, step, jnp.int32(0))


def coefficients(v0, v1, v2, drain):
    z = lax.broadcasted_iota(jnp.int32, v0.shape, v0.ndim - 1) & (NZ - 1)
    north = DISP - jnp.minimum(v0, 0.0)
    south = DISP + jnp.maximum(v0, 0.0)
    east = DISP - jnp.minimum(v1, 0.0)
    west = DISP + jnp.maximum(v1, 0.0)
    up = jnp.where(z == NZ - 1, 0.0, DISP - jnp.minimum(v2, 0.0))
    down = jnp.where(z == 0, 0.0, DISP + jnp.maximum(v2, 0.0))
    centre = ((north + south) + (east + west)) + ((up + down) + drain)
    return north, south, east, west, up, down, centre


def east_of(u, t, right, a, rows):
    here = pl.ds(a, rows)
    lo = lane_iota(rows) < NZ
    return pltpu.roll(jnp.where(lo, u[right, here, :], u[t, here, :]), NZ, 1)


def flux(u, coef, src, t, right, a, rows, west):
    cn, cs, ce, cw, cu, cd, cc = coef
    here = pl.ds(a, rows)
    mid = u[t, here, :]
    north = u[t, pl.ds(a + 1, rows), :]
    south = u[t, pl.ds(a - 1, rows), :]
    east = east_of(u, t, right, a, rows)
    upper = pltpu.roll(mid, LANES - 1, 1)
    lower = pltpu.roll(mid, 1, 1)
    plane = cn[t, here, :] * north + cs[t, here, :] * south
    plane = plane + (ce[t, here, :] * east + cw[t, here, :] * west)
    plane = plane + (cu[t, here, :] * upper + cd[t, here, :] * lower)
    return mid, plane + (src[t, here, :] - cc[t, here, :] * mid), east


def flux_back(w, coef, t, left, right, a, rows):
    cn, cs, ce, cw, cu, cd, cc = coef
    here = pl.ds(a, rows)
    above, below = pl.ds(a + 1, rows), pl.ds(a - 1, rows)
    lo = lane_iota(rows) < NZ
    mid = w[t, here, :]
    w_right, w_left = w[right, here, :], w[left, here, :]
    from_low = cw[right, here, :] * w_right + ce[t, here, :] * mid
    from_high = cw[t, here, :] * mid + ce[left, here, :] * w_left
    total = pltpu.roll(jnp.where(lo, from_low, from_high), NZ, 1)
    total = total + (cs[t, above, :] * w[t, above, :] + cn[t, below, :] * w[t, below, :])
    total = total + pltpu.roll(cd[t, here, :] * mid, LANES - 1, 1)
    total = total + pltpu.roll(cu[t, here, :] * mid, 1, 1)
    return total - cc[t, here, :] * mid


def sorb(u):
    return jnp.exp((FREUND - 1.0) * jnp.log(u))


def rate_of(kd, power):
    return STEP / (1.0 + BULK * kd * power)


def first_half(place, found, count, lines, xl, xr, stack_h,
               u0, fst, d1, rate, power, cn, cs, ce, cw, cu, cd, cc, src, msg_a, msg_b,
               stack, sems):
    loads = [
        pltpu.make_async_copy(stack_h.at[k], stack.at[k], sems.at[k]) for k in range(6)
    ]
    for load in loads:
        load.start()
    coef = (cn, cs, ce, cw, cu, cd, cc)
    own = pl.ds(BASE, ROWS)
    lines_of = lines.shape[1]
    for k in range(lines.shape[0]):
        for t in range(WT):
            u0[t, BASE + lines_of * k : BASE + lines_of * (k + 1), :] = lines[
                k, :, t * LANES : (t + 1) * LANES
            ]
    lo = lane_iota(ROWS) < NZ

    def third(ref, f, high):
        both = ref[7 + f // 2]
        if high:
            return jnp.where(lo, 0.0, both if f % 2 else pltpu.roll(both, NZ, 1))
        return jnp.where(lo, pltpu.roll(both, NZ, 1) if f % 2 else both, 0.0)

    for tile, fields in (
        (0, [third(xl, f, True) for f in range(6)]),
        (1, [xl[f] for f in range(6)]),
        (WT - 2, [xr[f] for f in range(6)]),
        (WT - 1, [third(xr, f, False) for f in range(6)]),
    ):
        for ref, val in zip(coef, coefficients(*fields[1:4], fields[5])):
            ref[tile, own, :] = val
        src[tile, own, :] = fields[4]
        rate[tile, own, :] = rate_of(fields[0], sorb(u0[tile, own, :]))

    @pl.when(place[0] == 0)
    def _():
        for ref in (u0, rate):
            ref[0:2, own, :] = jnp.zeros((2, ROWS, LANES), F32)

    @pl.when(place[1] == 0)
    def _():
        for ref in (u0, rate):
            ref[WT - 2 : WT, own, :] = jnp.zeros((2, ROWS, LANES), F32)

    for load in loads:
        load.wait()

    def prepare(t, carry):
        cols = pl.ds(pl.multiple_of(t * LANES, LANES), LANES)
        for r in range(0, ROWS, 8):
            rr, at = pl.ds(r, 8), pl.ds(BASE + r, 8)
            p = sorb(u0[t + 2, at, :])
            power[t, rr, :] = p
            rate[t + 2, at, :] = rate_of(stack[0, rr, cols], p)
            values = coefficients(
                stack[1, rr, cols], stack[2, rr, cols], stack[3, rr, cols], stack[5, rr, cols]
            )
            for ref, val in zip(coef, values):
                ref[t + 2, at, :] = val
            src[t + 2, at, :] = stack[4, rr, cols]
        return carry

    lax.fori_loop(0, TILES, prepare, 0, unroll=2)

    spans = range(BASE, BASE + ROWS, 8)

    def step(t, wests):
        right = jnp.minimum(t + 1, WT - 1)
        easts = []
        for a, west in zip(spans, wests):
            at = pl.ds(a, 8)
            mid, f, east = flux(u0, coef, src, t, right, a, 8, west)
            d = rate[t, at, :] * f
            d1[t, at, :] = d
            fst[t, at, :] = mid + d
            easts.append(east)
        return tuple(easts)

    zero = jnp.zeros((8, LANES), F32)
    lax.fori_loop(0, WT, step, (zero,) * len(spans), unroll=UNROLL)

    top = BASE + ROWS
    odd = place[4] == 1

    def send(at, row, up, low):
        msg_a[row, at] = jnp.where(odd, low, up)
        msg_b[row, at] = jnp.where(odd, up, low)

    for t in range(WT):
        at = pl.ds(t * LANES, LANES)
        send(at, slice(0, 2), u0[t, top - 2 : top, :], u0[t, BASE : BASE + 2, :])
        send(at, slice(2, 4), fst[t, top - 3 : top - 1, :], fst[t, BASE + 1 : BASE + 3, :])
    blank = jnp.zeros((1, LANES), F32)
    for k in range(16):
        at = pl.ds(WCOLS + (k % 4) * LANES, LANES)
        row = slice(k // 4, k // 4 + 1)
        side = xr if k % 2 else xl
        if k < 14:
            send(at, row, side[k // 2, ROWS - 1 : ROWS, :], side[k // 2, 0:1, :])
        else:
            send(at, row, blank, blank)


def second_half(place, found, count, xl, xr, yl, yh, msg_a, msg_b, kd_h, t_h, power,
                u0_in, fst_in, d1_in, rate_in, cn_in, cs_in, ce_in, cw_in, cu_in, cd_in, cc_in, src_in,
                kd_out_h, start_out_h,
                u0, fst, d1, rate, cn, cs, ce, cw, cu, cd, cc, src,
                kd, tgt, kd_out, start_out, halo, target, d2, mis, w, grad, w1, sems):
    loads = [
        pltpu.make_async_copy(a, b, sems.at[k, 0]) for k, (a, b) in enumerate(((kd_h, kd), (t_h, tgt)))
    ]
    for load in loads:
        load.start()
    coef = (cn, cs, ce, cw, cu, cd, cc)
    low8, high8 = slice(0, BASE), slice(BASE + ROWS, WR)
    own = pl.ds(BASE, ROWS)

    top = BASE + ROWS
    odd = place[4] == 1

    def arrived(row, at):
        one, two = msg_a[row, at], msg_b[row, at]
        return jnp.where(odd, one, two), jnp.where(odd, two, one)

    blank = jnp.zeros((16, LANES), F32)
    for f in range(7):
        for tile in (0, 1, WT - 2, WT - 1):
            halo[f, tile] = blank
        for t in range(TILES):
            at = pl.ds(t * LANES, LANES)
            halo[f, t + 2, 6:8, :] = yl[f, :, at]
            halo[f, t + 2, 8:10, :] = yh[f, :, at]
        for side, tile in ((0, 1), (1, WT - 2)):
            k = 2 * f + side
            low, high = arrived(slice(k // 4, k // 4 + 1), pl.ds(WCOLS + (k % 4) * LANES, LANES))
            halo[f, tile, 7:8, :] = low
            halo[f, tile, 8:9, :] = high
    for t in range(WT):
        at = pl.ds(t * LANES, LANES)
        low, high = arrived(slice(0, 4), at)
        u0[t, 6:8, :] = low[0:2]
        fst[t, 5:7, :] = low[2:4]
        u0[t, top : top + 2, :] = high[0:2]
        fst[t, top + 1 : top + 3, :] = high[2:4]

    def edges(t, carry):
        for a, to in ((0, low8), (8, high8)):
            at = pl.ds(a, 8)
            values = coefficients(halo[1, t, at, :], halo[2, t, at, :], halo[3, t, at, :], halo[5, t, at, :])
            for ref, val in zip(coef, values):
                ref[t, to, :] = val
            src[t, to, :] = halo[4, t, at, :]
            rate[t, to, :] = rate_of(halo[0, t, at, :], sorb(u0[t, to, :]))
            target[t, to, :] = halo[6, t, at, :]
        return carry

    lax.fori_loop(0, WT, edges, 0, unroll=6)

    zero8 = jnp.zeros((WT, BASE, LANES), F32)

    @pl.when(place[0] == 0)
    def _():
        rate[0:2] = jnp.zeros((2, WR, LANES), F32)
        u0[0:2] = jnp.zeros((2, WR, LANES), F32)

    @pl.when(place[1] == 0)
    def _():
        rate[WT - 2 : WT] = jnp.zeros((2, WR, LANES), F32)
        u0[WT - 2 : WT] = jnp.zeros((2, WR, LANES), F32)

    @pl.when(place[2] == 0)
    def _():
        rate[:, low8, :] = zero8
        u0[:, low8, :] = zero8
        fst[:, low8, :] = zero8

    @pl.when(place[3] == 0)
    def _():
        rate[:, high8, :] = zero8
        u0[:, high8, :] = zero8
        fst[:, high8, :] = zero8

    edge_spans = ((BASE - 4, BASE - 1), (top - 4, top - 1))

    def edge_step(t, wests):
        right = jnp.minimum(t + 1, WT - 1)
        easts = []
        for (a, r0), west in zip(edge_spans, wests):
            at = pl.ds(a, 8)
            row = lax.broadcasted_iota(jnp.int32, (8, LANES), 0) + a
            new = (row == r0) | (row == r0 + 1)
            mid, f, east = flux(u0, coef, src, t, right, a, 8, west)
            d = rate[t, at, :] * f
            d1[t, at, :] = jnp.where(new, d, d1[t, at, :])
            fst[t, at, :] = jnp.where(new, mid + d, fst[t, at, :])
            easts.append(east)
        return tuple(easts)

    zero = jnp.zeros((8, LANES), F32)
    lax.fori_loop(0, WT, edge_step, (zero, zero), unroll=6)

    loads[1].wait()

    def targets(t, carry):
        at = pl.ds(pl.multiple_of(t * LANES, LANES), LANES)
        target[t + 2, own, :] = tgt[:, at]
        return carry

    lax.fori_loop(0, TILES, targets, 0)
    target[1, own, :] = xl[6]
    target[WT - 2, own, :] = xr[6]

    spans = range(BASE - 4, BASE + ROWS + 4, 8)

    def step(t, wests):
        easts = []
        for a, west in zip(spans, wests):
            at = pl.ds(a, 8)
            mid, f, east = flux(fst, coef, src, t, t + 1, a, 8, west)
            rt = rate[t, at, :]
            d = rt * f
            d2[t, at, :] = d
            m = (mid + d) - target[t, at, :]
            mis[t, at, :] = m
            w[t, at, :] = m * rt
            easts.append(east)
        return tuple(easts)

    lax.fori_loop(1, WT - 1, step, tuple(east_of(fst, 0, 1, a, 8) for a in spans), unroll=UNROLL)

    lane = lax.broadcasted_iota(jnp.int32, (1, LANES), 1)

    def weigh(i, carry):
        code = found[i]
        row, col = code >> 16, (code >> 6) & 127
        hit = lane == (col & 1) * NZ + (code & (NZ - 1))
        tile = col >> 1
        at = pl.ds(row, 1)
        factor = jnp.where(hit, 1.0 + OUTLET_W, 1.0)
        mis[tile, at, :] = mis[tile, at, :] * factor
        w[tile, at, :] = w[tile, at, :] * factor
        return carry

    lax.fori_loop(0, count[0], weigh, 0)

    def back(t, carry):
        for a in spans:
            at = pl.ds(a, 8)
            g = mis[t, at, :] + flux_back(w, coef, t, t - 1, t + 1, a, 8)
            grad[t, at, :] = g
            w1[t, at, :] = g * rate[t, at, :]
        return carry

    lax.fori_loop(1, WT - 1, back, 0, unroll=UNROLL)
    loads[0].wait()

    def last(t, carry):
        cols = pl.ds(pl.multiple_of(t * LANES, LANES), LANES)
        tw = t + 2
        for r in range(0, ROWS, 8):
            a = BASE + r
            at, rr = pl.ds(a, 8), pl.ds(r, 8)
            g = grad[tw, at, :]
            start = g + flux_back(w1, coef, tw, tw - 1, tw + 1, a, 8)
            both = mis[tw, at, :] * d2[tw, at, :] + g * d1[tw, at, :]
            kdg = (both * rate[tw, at, :]) * (power[t, rr, :] * (-BULK / STEP))
            kd_out[rr, cols] = kdg
            start_out[rr, cols] = start + kdg * kd[rr, cols] * (FREUND - 1.0) / u0[tw, at, :]
        return carry

    parts = 4
    stores = []
    for k in range(parts):
        lax.fori_loop(k * TILES // parts, (k + 1) * TILES // parts, last, 0, unroll=UNROLL)
        cols = pl.ds(k * COLS // parts, COLS // parts)
        for a, b, n in ((kd_out, kd_out_h, 2), (start_out, start_out_h, 3)):
            stores.append(pltpu.make_async_copy(a.at[:, cols], b.at[:, cols], sems.at[n, k]))
            stores[-1].start()
    for store in stores:
        store.wait()


def params(mib):
    return pltpu.CompilerParams(vmem_limit_bytes=mib * MIB)


def shifts(axis):
    n = lax.axis_size(axis)
    up = [(i, i + 1) for i in range(n - 1)]
    return up, [(b, a) for a, b in up]


def per_device(checkpoint, sorption_kd, velocity, source, target, cell_type, outlets):
    n_gx = lax.axis_size("gx")
    gx, gy = lax.axis_index("gx"), lax.axis_index("gy")
    lines = pl.pallas_call(
        pack_lines,
        out_shape=jax.ShapeDtypeStruct((n_gx, checkpoint.shape[1], WCOLS), F32),
        in_specs=[HB],
        out_specs=VM,
        scratch_shapes=[pltpu.SemaphoreType.DMA],
        compiler_params=params(60),
        name="pack_lines",
    )(checkpoint)
    arrived = lax.all_to_all(lines, "gx", split_axis=0, concat_axis=0, tiled=True)

    side = jax.ShapeDtypeStruct((10, ROWS, LANES), F32)
    line = jax.ShapeDtypeStruct((7, 2, COLS), F32)
    blocks = 8
    part = COLS // blocks
    flat = pl.BlockSpec((ROWS, part), lambda i: (0, i))
    deep = lambda *lead: pl.BlockSpec(lead + (part,), lambda i: (0, 0, i))
    kept = pl.BlockSpec(side.shape, lambda i: (0, 0, 0))
    stack, to_left, to_right, to_low, to_high = pl.pallas_call(
        pack_fields,
        grid=(blocks,),
        out_shape=[jax.ShapeDtypeStruct((6, ROWS, COLS), F32), side, side, line, line],
        in_specs=[flat, deep(3, ROWS), flat, flat, flat],
        out_specs=[deep(6, ROWS), kept, kept, deep(7, 2), deep(7, 2)],
        compiler_params=params(60),
        name="pack_fields",
    )(sorption_kd, velocity, source, cell_type, target)
    x_up, x_down = shifts("gx")
    y_up, y_down = shifts("gy")
    xl = lax.ppermute(to_right, "gx", x_up)
    xr = lax.ppermute(to_left, "gx", x_down)
    yl = lax.ppermute(to_high, "gy", y_up)
    yh = lax.ppermute(to_low, "gy", y_down)

    row = (outlets >> 16) - gy * ROWS + BASE
    col = ((outlets >> 6) & 1023) - gx * (COLS // NZ) + 4
    inside = (row >= BASE - 2) & (row < BASE + ROWS + 2) & (col >= 2) & (col < 70)
    codes = jnp.where(inside, (row << 16) + (col << 6) + (outlets & (NZ - 1)), -1)
    found, count = pl.pallas_call(
        list_outlets,
        out_shape=[
            jax.ShapeDtypeStruct((outlets.shape[0],), jnp.int32),
            jax.ShapeDtypeStruct((1,), jnp.int32),
        ],
        in_specs=[SM],
        out_specs=[SM, SM],
        compiler_params=params(1),
        name="list_outlets",
    )(codes)

    n_gy = lax.axis_size("gy")
    edge = jnp.stack([gx, n_gx - 1 - gx, gy, n_gy - 1 - gy, gy % 2]).astype(jnp.int32)
    message = jax.ShapeDtypeStruct((4, MCOLS), F32)
    power = jax.ShapeDtypeStruct((TILES, ROWS, LANES), F32)
    u0, fst, d1, rate, power, *rest = pl.pallas_call(
        first_half,
        out_shape=[window()] * 4 + [power] + [window()] * 8 + [message] * 2,
        in_specs=[SM] * 3 + [VM] * 3 + [HB],
        out_specs=[VM] * 15,
        scratch_shapes=[pltpu.VMEM((6, ROWS, COLS), F32), pltpu.SemaphoreType.DMA((6,))],
        compiler_params=params(FIRST_MIB),
        name="first_half",
    )(edge, found, count, arrived, xl, xr, stack)
    coefs, (msg_a, msg_b) = rest[:8], rest[8:]
    got_a = lax.ppermute(msg_a, "gy", [(i, i + 1 - 2 * (i % 2)) for i in range(n_gy)])
    got_b = lax.ppermute(msg_b, "gy", [(i, (i - 1 + 2 * (i % 2)) % n_gy) for i in range(n_gy)])

    kept = (u0, fst, d1, rate, *coefs)
    plane = jax.ShapeDtypeStruct((ROWS, COLS), F32)
    work = pltpu.VMEM((WT, WR, LANES), F32)
    outs = pl.pallas_call(
        second_half,
        out_shape=[plane, plane] + [window()] * 12,
        in_specs=[SM] * 3 + [VM] * 6 + [HB] * 2 + [VM] * 13,
        out_specs=[HB] * 2 + [VM] * 12,
        input_output_aliases={12 + k: 2 + k for k in range(12)},
        scratch_shapes=[
            *[pltpu.VMEM((ROWS, COLS), F32)] * 4,
            pltpu.VMEM((7, WT, 16, LANES), F32),
            work, work, work, work, work, work,
            pltpu.SemaphoreType.DMA((4, 4)),
        ],
        compiler_params=params(24),
        name="second_half",
    )(edge, found, count, xl, xr, yl, yh, got_a, got_b, sorption_kd, target, power, *kept)
    return outs[0], outs[1]


def solution(mesh):
    return jax.shard_map(
        per_device,
        mesh=mesh,
        in_specs=(
            P("gy", "gx", None),
            P("gy", "gx"),
            P(None, "gy", "gx"),
            P("gy", "gx"),
            P("gy", "gx"),
            P("gy", "gx"),
            P(),
        ),
        out_specs=(P("gy", "gx"), P("gy", "gx")),
        check_vma=False,
    )
```

```python
import jax
import jax.numpy as jnp
from jax import lax
from jax.experimental import pallas as pl
from jax.experimental.pallas import tpu as pltpu
from jax.sharding import PartitionSpec as P

NZ = 64
BULK = 4.0
FREUND = 0.7
DISP = 0.1
DRAIN = 0.5
STEP = 0.4
OUTLET_W = 4.0

LANES = 128
ROWS = 64
TILES = 32
WT = TILES + 4
WR = 80
BASE = 8
COLS = TILES * LANES
WCOLS = WT * LANES
MCOLS = WCOLS + 4 * LANES
F32 = jnp.float32
MIB = 1 << 20
FIRST_MIB = 27
STACK = 6
UNROLL = 4
PACK_BLOCKS = 4


def places():
    gx, gy = lax.axis_index("gx"), lax.axis_index("gy")
    return (
        gx, lax.axis_size("gx") - 1 - gx, gy, lax.axis_size("gy") - 1 - gy,
        lax.rem(gy, 2), lax.rem(gx, 2),
    )


VM = pl.BlockSpec(memory_space=pltpu.VMEM)
SM = pl.BlockSpec(memory_space=pltpu.SMEM)
HB = pl.BlockSpec(memory_space=pltpu.HBM)


def window(dtype=F32):
    return jax.ShapeDtypeStruct((WT, WR, LANES), dtype)


def lane_iota(rows):
    return lax.broadcasted_iota(jnp.int32, (rows, LANES), 1)


def pack_lines(src, out, held, arrived, sent):
    n = out.shape[0]
    loads, stores = [], []
    for i in range(n):
        low = i * COLS - 2 * LANES
        high = low + WCOLS
        a, b = max(low, 0), min(high, n * COLS)
        at = a - low
        pieces = [(a, b, at)]
        if low < 0:
            pieces.append((0, 2 * LANES, 0))
        if high > n * COLS:
            pieces.append((n * COLS - 2 * LANES, n * COLS, WCOLS - 2 * LANES))
        loads.append([
            pltpu.make_async_copy(
                src.at[0, :, a:b], held.at[i, :, at : at + b - a], arrived.at[i, k]
            )
            for k, (a, b, at) in enumerate(pieces)
        ])
        stores.append(pltpu.make_async_copy(held.at[i], out.at[i], sent.at[i]))
    for group in loads:
        for c in group:
            c.start()
    for group, store in zip(loads, stores):
        for c in group:
            c.wait()
        store.start()
    for store in stores:
        store.wait()


def pack_fields(kd, vl, vr, vt, vb, s, c, tl, tr, tt, tb,
                stack, side_a, side_b, line_a, line_b):
    step, last = pl.program_id(0), pl.num_programs(0) - 1
    place = places()
    odd_x, odd_y = place[5] == 1, place[4] == 1
    rows = kd.shape[0]

    def fields(kd, v, s, kind, t):
        return (
            kd, *v,
            jnp.where(kind == 1, s, 0.0),
            jnp.where(kind == 2, DRAIN, 0.0).astype(F32),
            t,
        )

    stack[0] = kd[...]
    stack[1] = jnp.where(c[...] == 1, s[...], 0.0)
    stack[2] = jnp.where(c[...] == 2, DRAIN, 0.0).astype(F32)

    lo = lane_iota(rows) < NZ

    def layers(v, t, near, far, at, low_side):
        def tile(k):
            cols = slice(at + k * LANES, at + (k + 1) * LANES)
            edge = slice(k * LANES, (k + 1) * LANES)
            return fields(
                kd[:, cols], [v[d, :, edge] for d in range(3)], s[:, cols], c[:, cols], t[:, edge]
            )
        full, part = tile(near), tile(far)
        merged = []
        for p in range(3):
            first, second = part[2 * p], part[2 * p + 1]
            if low_side:
                second = pltpu.roll(second, NZ, 1)
            else:
                first = pltpu.roll(first, NZ, 1)
            merged.append(jnp.where(lo, first, second))
        return list(full) + merged

    low_side = layers(vl, tl, 0, 1, 0, True)
    high_side = layers(vr, tr, 1, 0, COLS - 2 * LANES, False)
    for f, (low, high) in enumerate(zip(low_side, high_side)):
        side_a[f] = jnp.where(odd_x, low, high)
        side_b[f] = jnp.where(odd_x, high, low)

    def lines(out, v, t, at, edge):
        part = slice(at, at + 2)
        e = slice(edge, edge + 2)
        for f, val in enumerate(
            fields(kd[part], [v[d, e] for d in range(3)], s[part], c[part], t[e])
        ):
            out[f] = val

    for parity, low_out, high_out in ((True, line_a, line_b), (False, line_b, line_a)):
        this = odd_y if parity else jnp.logical_not(odd_y)

        @pl.when((step == 0) & this)
        def _():
            lines(low_out, vt, tt, 0, 0)

        @pl.when((step == last) & this)
        def _():
            lines(high_out, vb, tb, rows - 2, 6)


def list_outlets(codes, found, count):
    unroll = 32

    def step(i, n):
        values = [codes[i * unroll + k] for k in range(unroll)]
        for value in values:
            found[n] = value
            n = n + 1 + (value >> 31)
        return n

    count[0] = lax.fori_loop(0, codes.shape[0] // unroll, step, jnp.int32(0))


def coefficients(v0, v1, v2, drain):
    z = lax.broadcasted_iota(jnp.int32, v0.shape, v0.ndim - 1) & (NZ - 1)
    north = DISP - jnp.minimum(v0, 0.0)
    south = DISP + jnp.maximum(v0, 0.0)
    east = DISP - jnp.minimum(v1, 0.0)
    west = DISP + jnp.maximum(v1, 0.0)
    up = jnp.where(z == NZ - 1, 0.0, DISP - jnp.minimum(v2, 0.0))
    down = jnp.where(z == 0, 0.0, DISP + jnp.maximum(v2, 0.0))
    centre = ((north + south) + (east + west)) + ((up + down) + drain)
    return north, south, east, west, up, down, centre


def east_of(u, t, right, a, rows):
    here = pl.ds(a, rows)
    lo = lane_iota(rows) < NZ
    return pltpu.roll(jnp.where(lo, u[right, here, :], u[t, here, :]), NZ, 1)


def flux(u, coef, src, t, right, a, rows, west):
    cn, cs, ce, cw, cu, cd, cc = coef
    here = pl.ds(a, rows)
    mid = u[t, here, :]
    north = u[t, pl.ds(a + 1, rows), :]
    south = u[t, pl.ds(a - 1, rows), :]
    east = east_of(u, t, right, a, rows)
    upper = pltpu.roll(mid, LANES - 1, 1)
    lower = pltpu.roll(mid, 1, 1)
    plane = cn[t, here, :] * north + cs[t, here, :] * south
    plane = plane + (ce[t, here, :] * east + cw[t, here, :] * west)
    plane = plane + (cu[t, here, :] * upper + cd[t, here, :] * lower)
    return mid, plane + (src[t, here, :] - cc[t, here, :] * mid), east


def flux_back(w, coef, t, left, right, a, rows):
    cn, cs, ce, cw, cu, cd, cc = coef
    here = pl.ds(a, rows)
    above, below = pl.ds(a + 1, rows), pl.ds(a - 1, rows)
    lo = lane_iota(rows) < NZ
    mid = w[t, here, :]
    w_right, w_left = w[right, here, :], w[left, here, :]
    from_low = cw[right, here, :] * w_right + ce[t, here, :] * mid
    from_high = cw[t, here, :] * mid + ce[left, here, :] * w_left
    total = pltpu.roll(jnp.where(lo, from_low, from_high), NZ, 1)
    total = total + (cs[t, above, :] * w[t, above, :] + cn[t, below, :] * w[t, below, :])
    total = total + pltpu.roll(cd[t, here, :] * mid, LANES - 1, 1)
    total = total + pltpu.roll(cu[t, here, :] * mid, 1, 1)
    return total - cc[t, here, :] * mid


def sorb(u):
    return jnp.exp((FREUND - 1.0) * jnp.log(u))


def rate_of(kd, power):
    return STEP / (1.0 + BULK * kd * power)


def first_half(found, count, lines, x_a, x_b, v_h, stack_h,
               u0, fst, d1, rate, power, cn, cs, ce, cw, cu, cd, cc, src, msg_a, msg_b,
               v, stack, sems):
    loads = [
        pltpu.make_async_copy(stack_h.at[0], stack.at[0], sems.at[0]),
        *[pltpu.make_async_copy(v_h.at[k], v.at[k], sems.at[k + 3]) for k in range(3)],
        pltpu.make_async_copy(stack_h.at[1], stack.at[1], sems.at[1]),
        pltpu.make_async_copy(stack_h.at[2], stack.at[2], sems.at[2]),
    ]
    for load in loads:
        load.start()
    coef = (cn, cs, ce, cw, cu, cd, cc)
    own = pl.ds(BASE, ROWS)
    lines_of = lines.shape[1]
    for k in range(lines.shape[0]):
        for t in range(WT):
            u0[t, BASE + lines_of * k : BASE + lines_of * (k + 1), :] = lines[
                k, :, t * LANES : (t + 1) * LANES
            ]
    lo = lane_iota(ROWS) < NZ

    place = places()
    odd_x = place[5] == 1

    def both(f, rows=slice(None)):
        one, two = x_a[f, rows], x_b[f, rows]
        return jnp.where(odd_x, one, two), jnp.where(odd_x, two, one)

    low_x, high_x = zip(*[both(f) for f in range(6)])
    low_3, high_3 = zip(*[both(f) for f in range(7, 10)])

    def third(parts, f, high):
        part = parts[f // 2]
        if high:
            return jnp.where(lo, 0.0, part if f % 2 else pltpu.roll(part, NZ, 1))
        return jnp.where(lo, pltpu.roll(part, NZ, 1) if f % 2 else part, 0.0)

    for tile, fields in (
        (0, [third(low_3, f, True) for f in range(6)]),
        (1, low_x),
        (WT - 2, high_x),
        (WT - 1, [third(high_3, f, False) for f in range(6)]),
    ):
        for ref, val in zip(coef, coefficients(*fields[1:4], fields[5])):
            ref[tile, own, :] = val
        src[tile, own, :] = fields[4]
        rate[tile, own, :] = rate_of(fields[0], sorb(u0[tile, own, :]))

    @pl.when(place[0] == 0)
    def _():
        for ref in (u0, rate):
            ref[0:2, own, :] = jnp.zeros((2, ROWS, LANES), F32)

    @pl.when(place[1] == 0)
    def _():
        for ref in (u0, rate):
            ref[WT - 2 : WT, own, :] = jnp.zeros((2, ROWS, LANES), F32)

    for load in loads:
        load.wait()

    def prepare(t, carry):
        cols = pl.ds(pl.multiple_of(t * LANES, LANES), LANES)
        for r in range(0, ROWS, 8):
            rr, at = pl.ds(r, 8), pl.ds(BASE + r, 8)
            p = sorb(u0[t + 2, at, :])
            power[t, rr, :] = p
            rate[t + 2, at, :] = rate_of(stack[0, rr, cols], p)
            values = coefficients(
                v[0, rr, cols], v[1, rr, cols], v[2, rr, cols], stack[2, rr, cols]
            )
            for ref, val in zip(coef, values):
                ref[t + 2, at, :] = val
            src[t + 2, at, :] = stack[1, rr, cols]
        return carry

    lax.fori_loop(0, TILES, prepare, 0, unroll=UNROLL)

    spans = range(BASE, BASE + ROWS, 8)

    def step(t, wests):
        right = jnp.minimum(t + 1, WT - 1)
        easts = []
        for a, west in zip(spans, wests):
            at = pl.ds(a, 8)
            mid, f, east = flux(u0, coef, src, t, right, a, 8, west)
            d = rate[t, at, :] * f
            d1[t, at, :] = d
            fst[t, at, :] = mid + d
            easts.append(east)
        return tuple(easts)

    first_west = tuple(east_of(u0, 0, 0, a, 8) for a in spans)
    lax.fori_loop(0, WT, step, first_west, unroll=UNROLL)

    top = BASE + ROWS
    odd = place[4] == 1

    def send(at, row, up, low):
        msg_a[row, at] = jnp.where(odd, low, up)
        msg_b[row, at] = jnp.where(odd, up, low)

    for t in range(WT):
        at = pl.ds(t * LANES, LANES)
        send(at, slice(0, 2), u0[t, top - 2 : top, :], u0[t, BASE : BASE + 2, :])
        send(at, slice(2, 4), fst[t, top - 3 : top - 1, :], fst[t, BASE + 1 : BASE + 3, :])
    blank = jnp.zeros((1, LANES), F32)
    for k in range(16):
        at = pl.ds(WCOLS + (k % 4) * LANES, LANES)
        row = slice(k // 4, k // 4 + 1)
        if k < 14:
            up = both(k // 2, slice(ROWS - 1, ROWS))[k % 2]
            send(at, row, up, both(k // 2, slice(0, 1))[k % 2])
        else:
            send(at, row, blank, blank)


def second_half(found, count, x_a, x_b, y_a, y_b, msg_a, msg_b, kd_h, t_h, power,
                u0_in, fst_in, d1_in, rate_in, cn_in, cs_in, ce_in, cw_in, cu_in, cd_in, cc_in, src_in,
                kd_out_h, start_out_h,
                u0, fst, d1, rate, cn, cs, ce, cw, cu, cd, cc, src,
                kd, tgt, kd_out, start_out, halo, target, d2, mis, w, grad, w1, sems):
    loads = [
        pltpu.make_async_copy(a, b, sems.at[k, 0]) for k, (a, b) in enumerate(((kd_h, kd), (t_h, tgt)))
    ]
    for load in loads:
        load.start()
    coef = (cn, cs, ce, cw, cu, cd, cc)
    low8, high8 = slice(0, BASE), slice(BASE + ROWS, WR)
    own = pl.ds(BASE, ROWS)

    top = BASE + ROWS
    place = places()
    odd = place[4] == 1

    def arrived(row, at):
        one, two = msg_a[row, at], msg_b[row, at]
        return jnp.where(odd, one, two), jnp.where(odd, two, one)

    for parity, y_low, y_high in ((True, y_a, y_b), (False, y_b, y_a)):

        @pl.when(odd if parity else jnp.logical_not(odd))
        def _():
            for f in range(7):
                for t in range(TILES):
                    at = pl.ds(t * LANES, LANES)
                    halo[f, t + 2, 6:8, :] = y_low[f, :, at]
                    halo[f, t + 2, 8:10, :] = y_high[f, :, at]

    blank = jnp.zeros((16, LANES), F32)
    for f in range(7):
        for tile in (0, 1, WT - 2, WT - 1):
            halo[f, tile] = blank
        for side, tile in ((0, 1), (1, WT - 2)):
            k = 2 * f + side
            low, high = arrived(slice(k // 4, k // 4 + 1), pl.ds(WCOLS + (k % 4) * LANES, LANES))
            halo[f, tile, 7:8, :] = low
            halo[f, tile, 8:9, :] = high
    for t in range(WT):
        at = pl.ds(t * LANES, LANES)
        low, high = arrived(slice(0, 4), at)
        u0[t, 6:8, :] = low[0:2]
        fst[t, 5:7, :] = low[2:4]
        u0[t, top : top + 2, :] = high[0:2]
        fst[t, top + 1 : top + 3, :] = high[2:4]

    def edges(t, carry):
        for a, to in ((0, low8), (8, high8)):
            at = pl.ds(a, 8)
            values = coefficients(halo[1, t, at, :], halo[2, t, at, :], halo[3, t, at, :], halo[5, t, at, :])
            for ref, val in zip(coef, values):
                ref[t, to, :] = val
            src[t, to, :] = halo[4, t, at, :]
            rate[t, to, :] = rate_of(halo[0, t, at, :], sorb(u0[t, to, :]))
            target[t, to, :] = halo[6, t, at, :]
        return carry

    lax.fori_loop(0, WT, edges, 0, unroll=6)

    zero8 = jnp.zeros((WT, BASE, LANES), F32)

    @pl.when(place[0] == 0)
    def _():
        rate[0:2] = jnp.zeros((2, WR, LANES), F32)
        u0[0:2] = jnp.zeros((2, WR, LANES), F32)

    @pl.when(place[1] == 0)
    def _():
        rate[WT - 2 : WT] = jnp.zeros((2, WR, LANES), F32)
        u0[WT - 2 : WT] = jnp.zeros((2, WR, LANES), F32)

    @pl.when(place[2] == 0)
    def _():
        rate[:, low8, :] = zero8
        u0[:, low8, :] = zero8
        fst[:, low8, :] = zero8

    @pl.when(place[3] == 0)
    def _():
        rate[:, high8, :] = zero8
        u0[:, high8, :] = zero8
        fst[:, high8, :] = zero8

    edge_spans = ((BASE - 4, BASE - 1), (top - 4, top - 1))

    def edge_step(t, wests):
        right = jnp.minimum(t + 1, WT - 1)
        easts = []
        for (a, r0), west in zip(edge_spans, wests):
            at = pl.ds(a, 8)
            row = lax.broadcasted_iota(jnp.int32, (8, LANES), 0) + a
            new = (row == r0) | (row == r0 + 1)
            mid, f, east = flux(u0, coef, src, t, right, a, 8, west)
            d = rate[t, at, :] * f
            d1[t, at, :] = jnp.where(new, d, d1[t, at, :])
            fst[t, at, :] = jnp.where(new, mid + d, fst[t, at, :])
            easts.append(east)
        return tuple(easts)

    first_west = tuple(east_of(u0, 0, 0, a, 8) for a, _ in edge_spans)
    lax.fori_loop(0, WT, edge_step, first_west, unroll=6)

    loads[1].wait()

    def targets(t, carry):
        at = pl.ds(pl.multiple_of(t * LANES, LANES), LANES)
        target[t + 2, own, :] = tgt[:, at]
        return carry

    lax.fori_loop(0, TILES, targets, 0)
    odd_x = place[5] == 1
    target[1, own, :] = jnp.where(odd_x, x_a[6], x_b[6])
    target[WT - 2, own, :] = jnp.where(odd_x, x_b[6], x_a[6])

    spans = range(BASE - 4, BASE + ROWS + 4, 8)

    def step(t, wests):
        easts = []
        for a, west in zip(spans, wests):
            at = pl.ds(a, 8)
            mid, f, east = flux(fst, coef, src, t, t + 1, a, 8, west)
            rt = rate[t, at, :]
            d = rt * f
            d2[t, at, :] = d
            m = (mid + d) - target[t, at, :]
            mis[t, at, :] = m
            w[t, at, :] = m * rt
            easts.append(east)
        return tuple(easts)

    lax.fori_loop(1, WT - 1, step, tuple(east_of(fst, 0, 1, a, 8) for a in spans), unroll=UNROLL)

    lane = lax.broadcasted_iota(jnp.int32, (1, LANES), 1)

    def weigh(i, carry):
        code = found[i]
        row, col = code >> 16, (code >> 6) & 127
        hit = lane == (col & 1) * NZ + (code & (NZ - 1))
        tile = col >> 1
        at = pl.ds(row, 1)
        factor = jnp.where(hit, 1.0 + OUTLET_W, 1.0)
        mis[tile, at, :] = mis[tile, at, :] * factor
        w[tile, at, :] = w[tile, at, :] * factor
        return carry

    lax.fori_loop(0, count[0], weigh, 0)

    def back(t, carry):
        for a in spans:
            at = pl.ds(a, 8)
            g = mis[t, at, :] + flux_back(w, coef, t, t - 1, t + 1, a, 8)
            grad[t, at, :] = g
            w1[t, at, :] = g * rate[t, at, :]
        return carry

    lax.fori_loop(1, WT - 1, back, 0, unroll=UNROLL)
    loads[0].wait()

    def last(t, carry):
        cols = pl.ds(pl.multiple_of(t * LANES, LANES), LANES)
        tw = t + 2
        for r in range(0, ROWS, 8):
            a = BASE + r
            at, rr = pl.ds(a, 8), pl.ds(r, 8)
            g = grad[tw, at, :]
            start = g + flux_back(w1, coef, tw, tw - 1, tw + 1, a, 8)
            both = mis[tw, at, :] * d2[tw, at, :] + g * d1[tw, at, :]
            kdg = (both * rate[tw, at, :]) * (power[t, rr, :] * (-BULK / STEP))
            kd_out[rr, cols] = kdg
            start_out[rr, cols] = start + kdg * kd[rr, cols] * (FREUND - 1.0) / u0[tw, at, :]
        return carry

    parts = 4
    stores = []
    for k in range(parts):
        lax.fori_loop(k * TILES // parts, (k + 1) * TILES // parts, last, 0, unroll=UNROLL)
        cols = pl.ds(k * COLS // parts, COLS // parts)
        for a, b, n in ((kd_out, kd_out_h, 2), (start_out, start_out_h, 3)):
            stores.append(pltpu.make_async_copy(a.at[:, cols], b.at[:, cols], sems.at[n, k]))
            stores[-1].start()
    for store in stores:
        store.wait()


def params(mib):
    return pltpu.CompilerParams(vmem_limit_bytes=mib * MIB)


def swap(a, b, axis):
    n = lax.axis_size(axis)

    def pairs(first):
        return [(i, j) for k in range(first, n - 1, 2) for i, j in ((k, k + 1), (k + 1, k))]

    return lax.ppermute(a, axis, pairs(0)), lax.ppermute(b, axis, pairs(1))


def per_device(checkpoint, sorption_kd, velocity, source, target, cell_type, outlets):
    n_gx = lax.axis_size("gx")
    gx, gy = lax.axis_index("gx"), lax.axis_index("gy")
    lines = pl.pallas_call(
        pack_lines,
        out_shape=jax.ShapeDtypeStruct((n_gx, checkpoint.shape[1], WCOLS), F32),
        in_specs=[HB],
        out_specs=HB,
        scratch_shapes=[
            pltpu.VMEM((n_gx, checkpoint.shape[1], WCOLS), F32),
            pltpu.SemaphoreType.DMA((n_gx, 2)),
            pltpu.SemaphoreType.DMA((n_gx,)),
        ],
        compiler_params=params(60),
        name="pack_lines",
    )(checkpoint)
    arrived = lax.all_to_all(lines, "gx", split_axis=0, concat_axis=0, tiled=True)

    side = jax.ShapeDtypeStruct((10, ROWS, LANES), F32)
    line = jax.ShapeDtypeStruct((7, 2, COLS), F32)
    row = (outlets >> 16) - gy * ROWS + BASE
    col = ((outlets >> 6) & 1023) - gx * (COLS // NZ) + 4
    inside = (row >= BASE - 2) & (row < BASE + ROWS + 2) & (col >= 2) & (col < 70)
    codes = jnp.where(inside, (row << 16) + (col << 6) + (outlets & (NZ - 1)), -1)
    rows = ROWS // PACK_BLOCKS
    flat = pl.BlockSpec((rows, COLS), lambda i: (i, 0))
    deep = lambda n, width: pl.BlockSpec((n, rows, width), lambda i: (0, i, 0))
    kept = pl.BlockSpec(line.shape, lambda i: (0, 0, 0))
    two = 2 * LANES
    ends = TILES // 2 - 1, ROWS // 8 - 1
    stack, side_a, side_b, line_a, line_b = pl.pallas_call(
        pack_fields,
        grid=(PACK_BLOCKS,),
        out_shape=[
            jax.ShapeDtypeStruct((STACK, ROWS, COLS), F32), side, side, line, line,
        ],
        in_specs=[
            flat,
            pl.BlockSpec((3, rows, two), lambda i: (0, i, 0)),
            pl.BlockSpec((3, rows, two), lambda i: (0, i, ends[0])),
            pl.BlockSpec((3, 8, COLS), lambda i: (0, 0, 0)),
            pl.BlockSpec((3, 8, COLS), lambda i: (0, ends[1], 0)),
            flat, flat,
            pl.BlockSpec((rows, two), lambda i: (i, 0)),
            pl.BlockSpec((rows, two), lambda i: (i, ends[0])),
            pl.BlockSpec((8, COLS), lambda i: (0, 0)),
            pl.BlockSpec((8, COLS), lambda i: (ends[1], 0)),
        ],
        out_specs=[deep(3, COLS), deep(10, LANES), deep(10, LANES), kept, kept],
        compiler_params=params(60),
        name="pack_fields",
    )(sorption_kd, *[velocity] * 4, source, cell_type, *[target] * 4)
    x_a, x_b = swap(side_a, side_b, "gx")
    y_a, y_b = swap(line_a, line_b, "gy")

    found, count = pl.pallas_call(
        list_outlets,
        out_shape=[
            jax.ShapeDtypeStruct((outlets.shape[0],), jnp.int32),
            jax.ShapeDtypeStruct((1,), jnp.int32),
        ],
        in_specs=[SM],
        out_specs=[SM, SM],
        compiler_params=params(1),
        name="list_outlets",
    )(codes)

    message = jax.ShapeDtypeStruct((4, MCOLS), F32)
    power = jax.ShapeDtypeStruct((TILES, ROWS, LANES), F32)
    u0, fst, d1, rate, power, *rest = pl.pallas_call(
        first_half,
        out_shape=[window()] * 4 + [power] + [window()] * 8 + [message] * 2,
        in_specs=[SM] * 2 + [VM] * 3 + [HB] * 2,
        out_specs=[VM] * 15,
        scratch_shapes=[*[pltpu.VMEM((3, ROWS, COLS), F32)] * 2, pltpu.SemaphoreType.DMA((6,))],
        compiler_params=params(FIRST_MIB),
        name="first_half",
    )(found, count, arrived, x_a, x_b, velocity, stack)
    coefs, (msg_a, msg_b) = rest[:8], rest[8:]
    got_a, got_b = swap(msg_a, msg_b, "gy")

    kept = (u0, fst, d1, rate, *coefs)
    plane = jax.ShapeDtypeStruct((ROWS, COLS), F32)
    work = pltpu.VMEM((WT, WR, LANES), F32)
    outs = pl.pallas_call(
        second_half,
        out_shape=[plane, plane] + [window()] * 12,
        in_specs=[SM] * 2 + [VM] * 6 + [HB] * 2 + [VM] * 13,
        out_specs=[HB] * 2 + [VM] * 12,
        input_output_aliases={11 + k: 2 + k for k in range(12)},
        scratch_shapes=[
            *[pltpu.VMEM((ROWS, COLS), F32)] * 4,
            pltpu.VMEM((7, WT, 16, LANES), F32),
            work, work, work, work, work, work,
            pltpu.SemaphoreType.DMA((4, 4)),
        ],
        compiler_params=params(24),
        name="second_half",
    )(found, count, x_a, x_b, y_a, y_b, got_a, got_b, sorption_kd, target, power, *kept)
    return outs[0], outs[1]


def solution(mesh):
    return jax.shard_map(
        per_device,
        mesh=mesh,
        in_specs=(
            P("gy", "gx", None),
            P("gy", "gx"),
            P(None, "gy", "gx"),
            P("gy", "gx"),
            P("gy", "gx"),
            P("gy", "gx"),
            P(),
        ),
        out_specs=(P("gy", "gx"), P("gy", "gx")),
        check_vma=False,
    )
```

```python
import jax
import jax.numpy as jnp
from jax import lax
from jax.experimental import pallas as pl
from jax.experimental.pallas import tpu as pltpu
from jax.sharding import PartitionSpec as P

NZ = 64
BULK = 4.0
FREUND = 0.7
DISP = 0.1
DRAIN = 0.5
STEP = 0.4
OUTLET_W = 4.0

LANES = 128
ROWS = 64
TILES = 32
WT = TILES + 4
WR = 80
BASE = 8
INNER = range(BASE + 4, BASE + ROWS - 8, 8)
BACK = range(INNER[0] + 8, INNER[-1], 8)
COLS = TILES * LANES
WCOLS = WT * LANES
MCOLS = WCOLS + 4 * LANES
F32 = jnp.float32
MIB = 1 << 20
FIRST_MIB = 27
STACK = 6
UNROLL = 4
PACK_BLOCKS = 4
PARTS = 4


def places():
    gx, gy = lax.axis_index("gx"), lax.axis_index("gy")
    return (
        gx, lax.axis_size("gx") - 1 - gx, gy, lax.axis_size("gy") - 1 - gy,
        lax.rem(gy, 2), lax.rem(gx, 2),
    )


VM = pl.BlockSpec(memory_space=pltpu.VMEM)
SM = pl.BlockSpec(memory_space=pltpu.SMEM)
HB = pl.BlockSpec(memory_space=pltpu.HBM)


def window(dtype=F32):
    return jax.ShapeDtypeStruct((WT, WR, LANES), dtype)


def lane_iota(rows):
    return lax.broadcasted_iota(jnp.int32, (rows, LANES), 1)


def pack_lines(src, out, held, arrived, sent):
    n = out.shape[0]
    loads, stores = [], []
    for i in range(n):
        low = i * COLS - 2 * LANES
        high = low + WCOLS
        a, b = max(low, 0), min(high, n * COLS)
        at = a - low
        pieces = [(a, b, at)]
        if low < 0:
            pieces.append((0, 2 * LANES, 0))
        if high > n * COLS:
            pieces.append((n * COLS - 2 * LANES, n * COLS, WCOLS - 2 * LANES))
        loads.append([
            pltpu.make_async_copy(
                src.at[0, :, a:b], held.at[i, :, at : at + b - a], arrived.at[i, k]
            )
            for k, (a, b, at) in enumerate(pieces)
        ])
        stores.append(pltpu.make_async_copy(held.at[i], out.at[i], sent.at[i]))
    for group in loads:
        for c in group:
            c.start()
    for group, store in zip(loads, stores):
        for c in group:
            c.wait()
        store.start()
    for store in stores:
        store.wait()


def all_fields(kd, v, s, c, t, at):
    kind = c[at]
    return (
        kd[at], *[v[(d, *at)] for d in range(3)],
        jnp.where(kind == 1, s[at], 0.0),
        jnp.where(kind == 2, DRAIN, 0.0).astype(F32),
        t[at],
    )


def pack_sides(kdl, kdr, vl, vr, sl, sr, cl, cr, tl, tr, side_a, side_b):
    odd = places()[5] == 1
    lo = lane_iota(ROWS) < NZ

    def layers(refs, near, far, low_side):
        def tile(k):
            return all_fields(*refs, (slice(None), slice(k * LANES, (k + 1) * LANES)))
        part = tile(far)
        merged = []
        for p in range(3):
            first, second = part[2 * p], part[2 * p + 1]
            if low_side:
                second = pltpu.roll(second, NZ, 1)
            else:
                first = pltpu.roll(first, NZ, 1)
            merged.append(jnp.where(lo, first, second))
        return list(tile(near)) + merged

    low_side = layers((kdl, vl, sl, cl, tl), 0, 1, True)
    high_side = layers((kdr, vr, sr, cr, tr), 1, 0, False)
    for f, (low, high) in enumerate(zip(low_side, high_side)):
        side_a[f] = jnp.where(odd, low, high)
        side_b[f] = jnp.where(odd, high, low)


def stack_fields(side, kd, s, c, kdt, kdb, vt, vb, st, sb, ct, cb, tt, tb, stack, line_a, line_b):
    stack[0] = kd[...]
    stack[1] = jnp.where(c[...] == 1, s[...], 0.0)
    stack[2] = jnp.where(c[...] == 2, DRAIN, 0.0).astype(F32)

    @pl.when(pl.program_id(0) == 0)
    def _():
        odd = places()[4] == 1
        low_line = all_fields(kdt, vt, st, ct, tt, (slice(0, 2), slice(None)))
        high_line = all_fields(kdb, vb, sb, cb, tb, (slice(6, 8), slice(None)))
        for f, (low, high) in enumerate(zip(low_line, high_line)):
            line_a[f] = jnp.where(odd, low, high)
            line_b[f] = jnp.where(odd, high, low)


def list_outlets(codes, found, count):
    unroll = 32

    def step(i, n):
        values = [codes[i * unroll + k] for k in range(unroll)]
        for value in values:
            found[n] = value
            n = n + 1 + (value >> 31)
        return n

    count[0] = lax.fori_loop(0, codes.shape[0] // unroll, step, jnp.int32(0))


def coefficients(v0, v1, v2, drain):
    z = lax.broadcasted_iota(jnp.int32, v0.shape, v0.ndim - 1) & (NZ - 1)
    north = DISP - jnp.minimum(v0, 0.0)
    south = DISP + jnp.maximum(v0, 0.0)
    east = DISP - jnp.minimum(v1, 0.0)
    west = DISP + jnp.maximum(v1, 0.0)
    up = jnp.where(z == NZ - 1, 0.0, DISP - jnp.minimum(v2, 0.0))
    down = jnp.where(z == 0, 0.0, DISP + jnp.maximum(v2, 0.0))
    centre = ((north + south) + (east + west)) + ((up + down) + drain)
    return north, south, east, west, up, down, centre


def east_of(u, t, right, a, rows):
    here = pl.ds(a, rows)
    lo = lane_iota(rows) < NZ
    return pltpu.roll(jnp.where(lo, u[right, here, :], u[t, here, :]), NZ, 1)


def flux(u, coef, src, t, right, a, rows, west):
    cn, cs, ce, cw, cu, cd, cc = coef
    here = pl.ds(a, rows)
    mid = u[t, here, :]
    north = u[t, pl.ds(a + 1, rows), :]
    south = u[t, pl.ds(a - 1, rows), :]
    east = east_of(u, t, right, a, rows)
    upper = pltpu.roll(mid, LANES - 1, 1)
    lower = pltpu.roll(mid, 1, 1)
    plane = cn[t, here, :] * north + cs[t, here, :] * south
    plane = plane + (ce[t, here, :] * east + cw[t, here, :] * west)
    plane = plane + (cu[t, here, :] * upper + cd[t, here, :] * lower)
    return mid, plane + (src[t, here, :] - cc[t, here, :] * mid), east


def flux_back(w, coef, t, left, right, a, rows):
    cn, cs, ce, cw, cu, cd, cc = coef
    here = pl.ds(a, rows)
    above, below = pl.ds(a + 1, rows), pl.ds(a - 1, rows)
    lo = lane_iota(rows) < NZ
    mid = w[t, here, :]
    w_right, w_left = w[right, here, :], w[left, here, :]
    from_low = cw[right, here, :] * w_right + ce[t, here, :] * mid
    from_high = cw[t, here, :] * mid + ce[left, here, :] * w_left
    total = pltpu.roll(jnp.where(lo, from_low, from_high), NZ, 1)
    total = total + (cs[t, above, :] * w[t, above, :] + cn[t, below, :] * w[t, below, :])
    total = total + pltpu.roll(cd[t, here, :] * mid, LANES - 1, 1)
    total = total + pltpu.roll(cu[t, here, :] * mid, 1, 1)
    return total - cc[t, here, :] * mid


def sorb(u):
    return jnp.exp((FREUND - 1.0) * jnp.log(u))


def rate_of(kd, power):
    return STEP / (1.0 + BULK * kd * power)


def first_half(found, count, lines, x_a, x_b, v_h, stack_h,
               u0, fst, d1, rate, power, cn, cs, ce, cw, cu, cd, cc, src, msg_a, msg_b,
               v, stack, sems):
    loads = []
    for k in range(PARTS):
        cols = pl.ds(k * COLS // PARTS, COLS // PARTS)
        loads.append([
            pltpu.make_async_copy(stack_h.at[0:3, :, cols], stack.at[:, :, cols], sems.at[2 * k]),
            pltpu.make_async_copy(v_h.at[:, :, cols], v.at[:, :, cols], sems.at[2 * k + 1]),
        ])
    for pair in loads:
        for load in pair:
            load.start()
    coef = (cn, cs, ce, cw, cu, cd, cc)
    own = pl.ds(BASE, ROWS)
    lines_of = lines.shape[1]
    for k in range(lines.shape[0]):
        for t in range(WT):
            u0[t, BASE + lines_of * k : BASE + lines_of * (k + 1), :] = lines[
                k, :, t * LANES : (t + 1) * LANES
            ]
    lo = lane_iota(ROWS) < NZ

    place = places()
    odd_x = place[5] == 1

    def both(f, rows=slice(None)):
        one, two = x_a[f, rows], x_b[f, rows]
        return jnp.where(odd_x, one, two), jnp.where(odd_x, two, one)

    low_x, high_x = zip(*[both(f) for f in range(6)])
    low_3, high_3 = zip(*[both(f) for f in range(7, 10)])

    def third(parts, f, high):
        part = parts[f // 2]
        if high:
            return jnp.where(lo, 0.0, part if f % 2 else pltpu.roll(part, NZ, 1))
        return jnp.where(lo, pltpu.roll(part, NZ, 1) if f % 2 else part, 0.0)

    for tile, fields in (
        (0, [third(low_3, f, True) for f in range(6)]),
        (1, low_x),
        (WT - 2, high_x),
        (WT - 1, [third(high_3, f, False) for f in range(6)]),
    ):
        for ref, val in zip(coef, coefficients(*fields[1:4], fields[5])):
            ref[tile, own, :] = val
        src[tile, own, :] = fields[4]
        rate[tile, own, :] = rate_of(fields[0], sorb(u0[tile, own, :]))

    @pl.when(place[0] == 0)
    def _():
        for ref in (u0, rate):
            ref[0:2, own, :] = jnp.zeros((2, ROWS, LANES), F32)

    @pl.when(place[1] == 0)
    def _():
        for ref in (u0, rate):
            ref[WT - 2 : WT, own, :] = jnp.zeros((2, ROWS, LANES), F32)

    def prepare(t, carry):
        cols = pl.ds(pl.multiple_of(t * LANES, LANES), LANES)
        for r in range(0, ROWS, 8):
            rr, at = pl.ds(r, 8), pl.ds(BASE + r, 8)
            p = sorb(u0[t + 2, at, :])
            power[t, rr, :] = p
            rate[t + 2, at, :] = rate_of(stack[0, rr, cols], p)
            values = coefficients(
                v[0, rr, cols], v[1, rr, cols], v[2, rr, cols], stack[2, rr, cols]
            )
            for ref, val in zip(coef, values):
                ref[t + 2, at, :] = val
            src[t + 2, at, :] = stack[1, rr, cols]
        return carry

    for k, pair in enumerate(loads):
        for load in pair:
            load.wait()
        lax.fori_loop(k * TILES // PARTS, (k + 1) * TILES // PARTS, prepare, 0, unroll=UNROLL)

    spans = range(BASE, BASE + ROWS, 8)

    def step(t, wests):
        right = jnp.minimum(t + 1, WT - 1)
        easts = []
        for a, west in zip(spans, wests):
            at = pl.ds(a, 8)
            mid, f, east = flux(u0, coef, src, t, right, a, 8, west)
            d = rate[t, at, :] * f
            d1[t, at, :] = d
            fst[t, at, :] = mid + d
            easts.append(east)
        return tuple(easts)

    first_west = tuple(east_of(u0, 0, 0, a, 8) for a in spans)
    lax.fori_loop(0, WT, step, first_west, unroll=UNROLL)

    top = BASE + ROWS
    odd = place[4] == 1

    def send(at, row, up, low):
        msg_a[row, at] = jnp.where(odd, low, up)
        msg_b[row, at] = jnp.where(odd, up, low)

    for t in range(WT):
        at = pl.ds(t * LANES, LANES)
        send(at, slice(0, 2), u0[t, top - 2 : top, :], u0[t, BASE : BASE + 2, :])
        send(at, slice(2, 4), fst[t, top - 3 : top - 1, :], fst[t, BASE + 1 : BASE + 3, :])
    blank = jnp.zeros((1, LANES), F32)
    for k in range(16):
        at = pl.ds(WCOLS + (k % 4) * LANES, LANES)
        row = slice(k // 4, k // 4 + 1)
        if k < 14:
            up = both(k // 2, slice(ROWS - 1, ROWS))[k % 2]
            send(at, row, up, both(k // 2, slice(0, 1))[k % 2])
        else:
            send(at, row, blank, blank)


def second_step(fst, coef, src, rate, target, d2, mis, w, spans):
    def step(t, wests):
        easts = []
        for a, west in zip(spans, wests):
            at = pl.ds(a, 8)
            mid, f, east = flux(fst, coef, src, t, t + 1, a, 8, west)
            rt = rate[t, at, :]
            d = rt * f
            d2[t, at, :] = d
            m = (mid + d) - target[t, at, :]
            mis[t, at, :] = m
            w[t, at, :] = m * rt
            easts.append(east)
        return tuple(easts)

    return step, tuple(east_of(fst, 0, 1, a, 8) for a in spans)


def weigh_outlets(found, count, mis, w, inner):
    lane = lax.broadcasted_iota(jnp.int32, (1, LANES), 1)

    def weigh(i, carry):
        code = found[i]
        row, col = code >> 16, (code >> 6) & 127
        within = (row >= INNER[0]) & (row < INNER[-1] + 8)
        at = pl.ds(row, 1)
        tile = col >> 1

        @pl.when(within if inner else jnp.logical_not(within))
        def _():
            hit = lane == (col & 1) * NZ + (code & (NZ - 1))
            factor = jnp.where(hit, 1.0 + OUTLET_W, 1.0)
            mis[tile, at, :] = mis[tile, at, :] * factor
            w[tile, at, :] = w[tile, at, :] * factor

        return carry

    lax.fori_loop(0, count[0], weigh, 0)


def adjoint_step(coef, rate, mis, w, grad, w1, spans):
    def back(t, carry):
        for a in spans:
            at = pl.ds(a, 8)
            g = mis[t, at, :] + flux_back(w, coef, t, t - 1, t + 1, a, 8)
            grad[t, at, :] = g
            w1[t, at, :] = g * rate[t, at, :]
        return carry

    return back


def middle(found, count, x_a, x_b, y_a, y_b, t_h, fst, rate,
           cn_in, cs_in, ce_in, cw_in, cu_in, cd_in, cc_in, src_in,
           cn, cs, ce, cw, cu, cd, cc, src, target, kd_edge, d2, mis, w, grad, w1,
           tgt, halo, sem):
    load = pltpu.make_async_copy(t_h, tgt, sem)
    load.start()
    coef = (cn, cs, ce, cw, cu, cd, cc)
    place = places()
    odd = place[4] == 1
    own = pl.ds(BASE, ROWS)

    for parity, y_low, y_high in ((True, y_a, y_b), (False, y_b, y_a)):

        @pl.when(odd if parity else jnp.logical_not(odd))
        def _():
            for f in range(7):
                for t in range(TILES):
                    at = pl.ds(t * LANES, LANES)
                    halo[f, t, 6:8, :] = y_low[f, :, at]
                    halo[f, t, 8:10, :] = y_high[f, :, at]

    def edges(t, carry):
        for a, to in ((0, slice(0, BASE)), (8, slice(BASE + ROWS, WR))):
            at = pl.ds(a, 8)
            values = coefficients(*[halo[f, t, at, :] for f in (1, 2, 3, 5)])
            for ref, val in zip(coef, values):
                ref[t + 2, to, :] = val
            src[t + 2, to, :] = halo[4, t, at, :]
            target[t + 2, to, :] = halo[6, t, at, :]
            kd_edge[t + 2, at, :] = halo[0, t, at, :]
        return carry

    lax.fori_loop(0, TILES, edges, 0, unroll=4)
    load.wait()

    def targets(t, carry):
        at = pl.ds(pl.multiple_of(t * LANES, LANES), LANES)
        target[t + 2, own, :] = tgt[:, at]
        return carry

    lax.fori_loop(0, TILES, targets, 0, unroll=2)
    odd_x = place[5] == 1
    target[1, own, :] = jnp.where(odd_x, x_a[6], x_b[6])
    target[WT - 2, own, :] = jnp.where(odd_x, x_b[6], x_a[6])

    step, start = second_step(fst, coef, src, rate, target, d2, mis, w, INNER)
    lax.fori_loop(1, WT - 1, step, start, unroll=UNROLL)
    weigh_outlets(found, count, mis, w, True)
    back = adjoint_step(coef, rate, mis, w, grad, w1, BACK)
    lax.fori_loop(1, WT - 1, back, 0, unroll=UNROLL)


def second_half(found, count, msg_a, msg_b, kd_h, power, kd_edge_in,
                u0_in, fst_in, d1_in, rate_in, cn_in, cs_in, ce_in, cw_in, cu_in, cd_in, cc_in, src_in,
                 target_in, d2_in, mis_in, w_in, grad_in, w1_in,
                kd_out_h, start_out_h,
                u0, fst, d1, rate, cn, cs, ce, cw, cu, cd, cc, src, target, d2, mis, w, grad, w1,
                kd, kd_out, start_out, halo, sems):
    load = pltpu.make_async_copy(kd_h, kd, sems.at[0, 0])
    load.start()
    coef = (cn, cs, ce, cw, cu, cd, cc)
    low8, high8 = slice(0, BASE), slice(BASE + ROWS, WR)
    top = BASE + ROWS
    place = places()
    odd = place[4] == 1

    def arrived(row, at):
        one, two = msg_a[row, at], msg_b[row, at]
        return jnp.where(odd, one, two), jnp.where(odd, two, one)

    for t in range(WT):
        at = pl.ds(t * LANES, LANES)
        low, high = arrived(slice(0, 4), at)
        u0[t, 6:8, :] = low[0:2]
        fst[t, 5:7, :] = low[2:4]
        u0[t, top : top + 2, :] = high[0:2]
        fst[t, top + 1 : top + 3, :] = high[2:4]

    for f in range(7):
        for n in range(4):
            halo[f, n] = jnp.zeros((16, LANES), F32)
        for side, n in ((0, 1), (1, 2)):
            k = 2 * f + side
            low, high = arrived(slice(k // 4, k // 4 + 1), pl.ds(WCOLS + (k % 4) * LANES, LANES))
            halo[f, n, 7:8, :] = low
            halo[f, n, 8:9, :] = high
    for n, t in enumerate((0, 1, WT - 2, WT - 1)):
        for a, to in ((0, low8), (8, high8)):
            at = pl.ds(a, 8)
            values = coefficients(*[halo[f, n, at, :] for f in (1, 2, 3, 5)])
            for ref, val in zip(coef, values):
                ref[t, to, :] = val
            src[t, to, :] = halo[4, n, at, :]
            target[t, to, :] = halo[6, n, at, :]
            rate[t, to, :] = rate_of(halo[0, n, at, :], sorb(u0[t, to, :]))

    def edges(t, carry):
        for a, to in ((0, low8), (8, high8)):
            rate[t, to, :] = rate_of(kd_edge_in[t, pl.ds(a, 8), :], sorb(u0[t, to, :]))
        return carry

    lax.fori_loop(2, WT - 2, edges, 0, unroll=8)

    zero8 = jnp.zeros((WT, BASE, LANES), F32)
    edge_rows = (low8, high8)

    @pl.when(place[0] == 0)
    def _():
        for to in edge_rows:
            rate[0:2, to, :] = zero8[:2]
            u0[0:2, to, :] = zero8[:2]

    @pl.when(place[1] == 0)
    def _():
        for to in edge_rows:
            rate[WT - 2 : WT, to, :] = zero8[:2]
            u0[WT - 2 : WT, to, :] = zero8[:2]

    @pl.when(place[2] == 0)
    def _():
        rate[:, low8, :] = zero8
        u0[:, low8, :] = zero8
        fst[:, low8, :] = zero8

    @pl.when(place[3] == 0)
    def _():
        rate[:, high8, :] = zero8
        u0[:, high8, :] = zero8
        fst[:, high8, :] = zero8

    edge_spans = ((BASE - 4, BASE - 1), (top - 4, top - 1))

    def edge_step(t, wests):
        right = jnp.minimum(t + 1, WT - 1)
        easts = []
        for (a, r0), west in zip(edge_spans, wests):
            at = pl.ds(a, 8)
            row = lax.broadcasted_iota(jnp.int32, (8, LANES), 0) + a
            new = (row == r0) | (row == r0 + 1)
            mid, f, east = flux(u0, coef, src, t, right, a, 8, west)
            d = rate[t, at, :] * f
            d1[t, at, :] = jnp.where(new, d, d1[t, at, :])
            fst[t, at, :] = jnp.where(new, mid + d, fst[t, at, :])
            easts.append(east)
        return tuple(easts)

    first_west = tuple(east_of(u0, 0, 0, a, 8) for a, _ in edge_spans)
    lax.fori_loop(0, WT, edge_step, first_west, unroll=12)

    spans = range(BASE - 4, BASE + ROWS + 4, 8)
    outer = [a for a in spans if a not in INNER]
    step, start = second_step(fst, coef, src, rate, target, d2, mis, w, outer)
    lax.fori_loop(1, WT - 1, step, start, unroll=9)

    weigh_outlets(found, count, mis, w, False)
    back = adjoint_step(coef, rate, mis, w, grad, w1, [a for a in spans if a not in BACK])
    lax.fori_loop(1, WT - 1, back, 0, unroll=UNROLL)
    load.wait()

    def last(t, carry):
        cols = pl.ds(pl.multiple_of(t * LANES, LANES), LANES)
        tw = t + 2
        for r in range(0, ROWS, 8):
            a = BASE + r
            at, rr = pl.ds(a, 8), pl.ds(r, 8)
            g = grad[tw, at, :]
            start = g + flux_back(w1, coef, tw, tw - 1, tw + 1, a, 8)
            both = mis[tw, at, :] * d2[tw, at, :] + g * d1[tw, at, :]
            kdg = (both * rate[tw, at, :]) * (power[t, rr, :] * (-BULK / STEP))
            kd_out[rr, cols] = kdg
            start_out[rr, cols] = start + kdg * kd[rr, cols] * (FREUND - 1.0) / u0[tw, at, :]
        return carry

    parts = PARTS
    stores = []
    for k in range(parts):
        lax.fori_loop(k * TILES // parts, (k + 1) * TILES // parts, last, 0, unroll=UNROLL)
        cols = pl.ds(k * COLS // parts, COLS // parts)
        for a, b, n in ((kd_out, kd_out_h, 2), (start_out, start_out_h, 3)):
            stores.append(pltpu.make_async_copy(a.at[:, cols], b.at[:, cols], sems.at[n, k]))
            stores[-1].start()
    for store in stores:
        store.wait()


def params(mib):
    return pltpu.CompilerParams(vmem_limit_bytes=mib * MIB)


def swap(a, b, axis):
    n = lax.axis_size(axis)

    def pairs(first):
        return [(i, j) for k in range(first, n - 1, 2) for i, j in ((k, k + 1), (k + 1, k))]

    return lax.ppermute(a, axis, pairs(0)), lax.ppermute(b, axis, pairs(1))


def per_device(checkpoint, sorption_kd, velocity, source, target, cell_type, outlets):
    n_gx = lax.axis_size("gx")
    gx, gy = lax.axis_index("gx"), lax.axis_index("gy")
    lines = pl.pallas_call(
        pack_lines,
        out_shape=jax.ShapeDtypeStruct((n_gx, checkpoint.shape[1], WCOLS), F32),
        in_specs=[HB],
        out_specs=HB,
        scratch_shapes=[
            pltpu.VMEM((n_gx, checkpoint.shape[1], WCOLS), F32),
            pltpu.SemaphoreType.DMA((n_gx, 2)),
            pltpu.SemaphoreType.DMA((n_gx,)),
        ],
        compiler_params=params(60),
        name="pack_lines",
    )(checkpoint)
    arrived = lax.all_to_all(lines, "gx", split_axis=0, concat_axis=0, tiled=True)

    side = jax.ShapeDtypeStruct((10, ROWS, LANES), F32)
    line = jax.ShapeDtypeStruct((7, 2, COLS), F32)
    row = (outlets >> 16) - gy * ROWS + BASE
    col = ((outlets >> 6) & 1023) - gx * (COLS // NZ) + 4
    inside = (row >= BASE - 2) & (row < BASE + ROWS + 2) & (col >= 2) & (col < 70)
    codes = jnp.where(inside, (row << 16) + (col << 6) + (outlets & (NZ - 1)), -1)
    rows = ROWS // PACK_BLOCKS
    flat = pl.BlockSpec((rows, COLS), lambda i: (i, 0))
    two = 2 * LANES

    def block_specs(lead, *blocks):
        return [
            pl.BlockSpec(lead + shape, lambda i, at=at: (0,) * len(lead) + at) for shape, at in blocks
        ]

    sides = ((ROWS, two), (0, 0)), ((ROWS, two), (0, TILES // 2 - 1))
    ends = ((8, COLS), (0, 0)), ((8, COLS), (ROWS // 8 - 1, 0))
    fields = (sorption_kd, velocity, source, cell_type, target)
    twice = [f for f in fields for _ in range(2)]

    def specs(blocks):
        return [b for f in fields for b in block_specs((3,) if f.ndim == 3 else (), *blocks)]

    whole = lambda a: pl.BlockSpec(a.shape, lambda i: (0, 0, 0))
    side_a, side_b = pl.pallas_call(
        pack_sides,
        grid=(1,),
        out_shape=[side, side],
        in_specs=specs(sides),
        out_specs=[whole(side), whole(side)],
        compiler_params=params(60),
        name="pack_sides",
    )(*twice)
    stack, line_a, line_b = pl.pallas_call(
        stack_fields,
        grid=(PACK_BLOCKS,),
        out_shape=[jax.ShapeDtypeStruct((STACK, ROWS, COLS), F32), line, line],
        in_specs=[HB, flat, flat, flat] + specs(ends),
        out_specs=[pl.BlockSpec((3, rows, COLS), lambda i: (0, i, 0)), whole(line), whole(line)],
        compiler_params=params(60),
        name="stack_fields",
    )(side_a, sorption_kd, source, cell_type, *twice)
    x_a, x_b = swap(side_a, side_b, "gx")
    y_a, y_b = swap(line_a, line_b, "gy")

    found, count = pl.pallas_call(
        list_outlets,
        out_shape=[
            jax.ShapeDtypeStruct((outlets.shape[0],), jnp.int32),
            jax.ShapeDtypeStruct((1,), jnp.int32),
        ],
        in_specs=[SM],
        out_specs=[SM, SM],
        compiler_params=params(1),
        name="list_outlets",
    )(codes)

    message = jax.ShapeDtypeStruct((4, MCOLS), F32)
    power = jax.ShapeDtypeStruct((TILES, ROWS, LANES), F32)
    u0, fst, d1, rate, power, *rest = pl.pallas_call(
        first_half,
        out_shape=[window()] * 4 + [power] + [window()] * 8 + [message] * 2,
        in_specs=[SM] * 2 + [VM] * 3 + [HB] * 2,
        out_specs=[VM] * 15,
        scratch_shapes=[*[pltpu.VMEM((3, ROWS, COLS), F32)] * 2, pltpu.SemaphoreType.DMA((2 * PARTS,))],
        compiler_params=params(FIRST_MIB),
        name="first_half",
    )(found, count, arrived, x_a, x_b, velocity, stack)
    coefs, (msg_a, msg_b) = rest[:8], rest[8:]
    got_a, got_b = swap(msg_a, msg_b, "gy")

    edge_kd = jax.ShapeDtypeStruct((WT, 16, LANES), F32)
    *coefs, aim, kd_edge, d2, mis, w, grad, w1 = pl.pallas_call(
        middle,
        out_shape=[window()] * 9 + [edge_kd] + [window()] * 5,
        in_specs=[SM] * 2 + [VM] * 4 + [HB] + [VM] * 10,
        out_specs=[VM] * 15,
        input_output_aliases={9 + k: k for k in range(8)},
        scratch_shapes=[
            pltpu.VMEM((ROWS, COLS), F32),
            pltpu.VMEM((7, TILES, 16, LANES), F32),
            pltpu.SemaphoreType.DMA,
        ],
        compiler_params=params(8),
        name="middle",
    )(found, count, x_a, x_b, y_a, y_b, target, fst, rate, *coefs)

    kept = (u0, fst, d1, rate, *coefs, aim, d2, mis, w, grad, w1)
    plane = jax.ShapeDtypeStruct((ROWS, COLS), F32)
    outs = pl.pallas_call(
        second_half,
        out_shape=[plane, plane] + [window()] * 18,
        in_specs=[SM] * 2 + [VM] * 2 + [HB] + [VM] * 20,
        out_specs=[HB] * 2 + [VM] * 18,
        input_output_aliases={7 + k: 2 + k for k in range(18)},
        scratch_shapes=[
            *[pltpu.VMEM((ROWS, COLS), F32)] * 3,
            pltpu.VMEM((7, 4, 16, LANES), F32),
            pltpu.SemaphoreType.DMA((4, 4)),
        ],
        compiler_params=params(12),
        name="second_half",
    )(found, count, got_a, got_b, sorption_kd, power, kd_edge, *kept)
    return outs[0], outs[1]


def solution(mesh):
    return jax.shard_map(
        per_device,
        mesh=mesh,
        in_specs=(
            P("gy", "gx", None),
            P("gy", "gx"),
            P(None, "gy", "gx"),
            P("gy", "gx"),
            P("gy", "gx"),
            P("gy", "gx"),
            P(),
        ),
        out_specs=(P("gy", "gx"), P("gy", "gx")),
        check_vma=False,
    )
```

```python
import jax
import jax.numpy as jnp
from jax import lax
from jax.experimental import pallas as pl
from jax.experimental.pallas import tpu as pltpu
from jax.sharding import PartitionSpec as P

NZ = 64
BULK = 4.0
FREUND = 0.7
DISP = 0.1
DRAIN = 0.5
STEP = 0.4
OUTLET_W = 4.0

LANES = 128
ROWS = 64
TILES = 32
WT = TILES + 4
WR = 80
BASE = 8
INNER = range(BASE + 4, BASE + ROWS - 8, 8)
BACK = range(INNER[0] + 8, INNER[-1], 8)
COLS = TILES * LANES
WCOLS = WT * LANES
MCOLS = WCOLS + 4 * LANES
F32 = jnp.float32
MIB = 1 << 20
FIRST_MIB = 27
STACK = 6
UNROLL = 8
PACK_BLOCKS = 4
PARTS = 4


def places():
    gx, gy = lax.axis_index("gx"), lax.axis_index("gy")
    return (
        gx, lax.axis_size("gx") - 1 - gx, gy, lax.axis_size("gy") - 1 - gy,
        lax.rem(gy, 2), lax.rem(gx, 2),
    )


VM = pl.BlockSpec(memory_space=pltpu.VMEM)
SM = pl.BlockSpec(memory_space=pltpu.SMEM)
HB = pl.BlockSpec(memory_space=pltpu.HBM)


def window(dtype=F32):
    return jax.ShapeDtypeStruct((WT, WR, LANES), dtype)


def lane_iota(rows):
    return lax.broadcasted_iota(jnp.int32, (rows, LANES), 1)


def pack_lines(src, out, held, arrived, sent):
    n = out.shape[0]
    loads, stores = [], []
    for i in range(n):
        low = i * COLS - 2 * LANES
        high = low + WCOLS
        a, b = max(low, 0), min(high, n * COLS)
        at = a - low
        pieces = [(a, b, at)]
        if low < 0:
            pieces.append((0, 2 * LANES, 0))
        if high > n * COLS:
            pieces.append((n * COLS - 2 * LANES, n * COLS, WCOLS - 2 * LANES))
        loads.append([
            pltpu.make_async_copy(
                src.at[0, :, a:b], held.at[i, :, at : at + b - a], arrived.at[i, k]
            )
            for k, (a, b, at) in enumerate(pieces)
        ])
        stores.append(pltpu.make_async_copy(held.at[i], out.at[i], sent.at[i]))
    for group in loads:
        for c in group:
            c.start()
    for group, store in zip(loads, stores):
        for c in group:
            c.wait()
        store.start()
    for store in stores:
        store.wait()


def all_fields(kd, v, s, c, t, at):
    kind = c[at]
    return (
        kd[at], *[v[(d, *at)] for d in range(3)],
        jnp.where(kind == 1, s[at], 0.0),
        jnp.where(kind == 2, DRAIN, 0.0).astype(F32),
        t[at],
    )


def pack_sides(kdl, kdr, vl, vr, sl, sr, cl, cr, tl, tr, side_a, side_b):
    odd = places()[5] == 1
    lo = lane_iota(ROWS) < NZ

    def layers(refs, near, far, low_side):
        def tile(k):
            return all_fields(*refs, (slice(None), slice(k * LANES, (k + 1) * LANES)))
        part = tile(far)
        merged = []
        for p in range(3):
            first, second = part[2 * p], part[2 * p + 1]
            if low_side:
                second = pltpu.roll(second, NZ, 1)
            else:
                first = pltpu.roll(first, NZ, 1)
            merged.append(jnp.where(lo, first, second))
        return list(tile(near)) + merged

    low_side = layers((kdl, vl, sl, cl, tl), 0, 1, True)
    high_side = layers((kdr, vr, sr, cr, tr), 1, 0, False)
    for f, (low, high) in enumerate(zip(low_side, high_side)):
        side_a[f] = jnp.where(odd, low, high)
        side_b[f] = jnp.where(odd, high, low)


def stack_fields(side, codes, code_rows, kd, s, c, kdt, kdb, vt, vb, st, sb, ct, cb, tt, tb,
                 stack, line_a, line_b, found, count):
    stack[0] = kd[...]
    stack[1] = jnp.where(c[...] == 1, s[...], 0.0)
    stack[2] = jnp.where(c[...] == 2, DRAIN, 0.0).astype(F32)

    @pl.when(pl.program_id(0) == 0)
    def _():
        odd = places()[4] == 1
        low_line = all_fields(kdt, vt, st, ct, tt, (slice(0, 2), slice(None)))
        high_line = all_fields(kdb, vb, sb, cb, tb, (slice(6, 8), slice(None)))
        for f, (low, high) in enumerate(zip(low_line, high_line)):
            line_a[f] = jnp.where(odd, low, high)
            line_b[f] = jnp.where(odd, high, low)


    @pl.when(pl.program_id(0) == 0)
    def _():
        count[0] = 0

    unroll = 32
    share = code_rows.shape[0] // PACK_BLOCKS
    for k in range(share):
        row = pl.program_id(0) * share + k

        @pl.when(jnp.max(code_rows[pl.ds(row, 1), :].astype(F32)) >= 0.0)
        def _():
            def compact(i, n):
                values = [codes[row * LANES + i * unroll + j] for j in range(unroll)]
                for value in values:
                    found[n] = value
                    n = n + 1 + (value >> 31)
                return n

            count[0] = lax.fori_loop(0, LANES // unroll, compact, count[0])


def coefficients(v0, v1, v2, drain):
    z = lax.broadcasted_iota(jnp.int32, v0.shape, v0.ndim - 1) & (NZ - 1)
    north = DISP - jnp.minimum(v0, 0.0)
    south = DISP + jnp.maximum(v0, 0.0)
    east = DISP - jnp.minimum(v1, 0.0)
    west = DISP + jnp.maximum(v1, 0.0)
    up = jnp.where(z == NZ - 1, 0.0, DISP - jnp.minimum(v2, 0.0))
    down = jnp.where(z == 0, 0.0, DISP + jnp.maximum(v2, 0.0))
    centre = ((north + south) + (east + west)) + ((up + down) + drain)
    return north, south, east, west, up, down, centre


def east_of(u, t, right, a, rows):
    here = pl.ds(a, rows)
    lo = lane_iota(rows) < NZ
    return pltpu.roll(jnp.where(lo, u[right, here, :], u[t, here, :]), NZ, 1)


def flux(u, coef, src, t, right, a, rows, west):
    cn, cs, ce, cw, cu, cd, cc = coef
    here = pl.ds(a, rows)
    mid = u[t, here, :]
    north = u[t, pl.ds(a + 1, rows), :]
    south = u[t, pl.ds(a - 1, rows), :]
    east = east_of(u, t, right, a, rows)
    upper = pltpu.roll(mid, LANES - 1, 1)
    lower = pltpu.roll(mid, 1, 1)
    plane = cn[t, here, :] * north + cs[t, here, :] * south
    plane = plane + (ce[t, here, :] * east + cw[t, here, :] * west)
    plane = plane + (cu[t, here, :] * upper + cd[t, here, :] * lower)
    return mid, plane + (src[t, here, :] - cc[t, here, :] * mid), east


def flux_back(w, coef, t, left, right, a, rows):
    cn, cs, ce, cw, cu, cd, cc = coef
    here = pl.ds(a, rows)
    above, below = pl.ds(a + 1, rows), pl.ds(a - 1, rows)
    lo = lane_iota(rows) < NZ
    mid = w[t, here, :]
    w_right, w_left = w[right, here, :], w[left, here, :]
    from_low = cw[right, here, :] * w_right + ce[t, here, :] * mid
    from_high = cw[t, here, :] * mid + ce[left, here, :] * w_left
    total = pltpu.roll(jnp.where(lo, from_low, from_high), NZ, 1)
    total = total + (cs[t, above, :] * w[t, above, :] + cn[t, below, :] * w[t, below, :])
    total = total + pltpu.roll(cd[t, here, :] * mid, LANES - 1, 1)
    total = total + pltpu.roll(cu[t, here, :] * mid, 1, 1)
    return total - cc[t, here, :] * mid


def sorb(u):
    return jnp.exp((FREUND - 1.0) * jnp.log(u))


def rate_of(kd, power):
    return STEP / (1.0 + BULK * kd * power)


def first_half(lines, x_a, x_b, v_h, stack_h,
               u0, fst, d1, rate, power, cn, cs, ce, cw, cu, cd, cc, src, msg_a, msg_b,
               v, stack, sems):
    loads = []
    for k in range(PARTS):
        cols = pl.ds(k * COLS // PARTS, COLS // PARTS)
        loads.append([
            pltpu.make_async_copy(stack_h.at[0:3, :, cols], stack.at[:, :, cols], sems.at[2 * k]),
            pltpu.make_async_copy(v_h.at[:, :, cols], v.at[:, :, cols], sems.at[2 * k + 1]),
        ])
    for pair in loads:
        for load in pair:
            load.start()
    coef = (cn, cs, ce, cw, cu, cd, cc)
    own = pl.ds(BASE, ROWS)
    lines_of = lines.shape[1]
    for k in range(lines.shape[0]):
        for t in range(WT):
            u0[t, BASE + lines_of * k : BASE + lines_of * (k + 1), :] = lines[
                k, :, t * LANES : (t + 1) * LANES
            ]
    lo = lane_iota(ROWS) < NZ

    place = places()
    odd_x = place[5] == 1

    def both(f, rows=slice(None)):
        one, two = x_a[f, rows], x_b[f, rows]
        return jnp.where(odd_x, one, two), jnp.where(odd_x, two, one)

    low_x, high_x = zip(*[both(f) for f in range(6)])
    low_3, high_3 = zip(*[both(f) for f in range(7, 10)])

    def third(parts, f, high):
        part = parts[f // 2]
        if high:
            return jnp.where(lo, 0.0, part if f % 2 else pltpu.roll(part, NZ, 1))
        return jnp.where(lo, pltpu.roll(part, NZ, 1) if f % 2 else part, 0.0)

    for tile, fields in (
        (0, [third(low_3, f, True) for f in range(6)]),
        (1, low_x),
        (WT - 2, high_x),
        (WT - 1, [third(high_3, f, False) for f in range(6)]),
    ):
        for ref, val in zip(coef, coefficients(*fields[1:4], fields[5])):
            ref[tile, own, :] = val
        src[tile, own, :] = fields[4]
        rate[tile, own, :] = rate_of(fields[0], sorb(u0[tile, own, :]))

    @pl.when(place[0] == 0)
    def _():
        for ref in (u0, rate):
            ref[0:2, own, :] = jnp.zeros((2, ROWS, LANES), F32)

    @pl.when(place[1] == 0)
    def _():
        for ref in (u0, rate):
            ref[WT - 2 : WT, own, :] = jnp.zeros((2, ROWS, LANES), F32)

    def prepare(t, carry):
        cols = pl.ds(pl.multiple_of(t * LANES, LANES), LANES)
        for r in range(0, ROWS, 8):
            rr, at = pl.ds(r, 8), pl.ds(BASE + r, 8)
            p = sorb(u0[t + 2, at, :])
            power[t, rr, :] = p
            rate[t + 2, at, :] = rate_of(stack[0, rr, cols], p)
            values = coefficients(
                v[0, rr, cols], v[1, rr, cols], v[2, rr, cols], stack[2, rr, cols]
            )
            for ref, val in zip(coef, values):
                ref[t + 2, at, :] = val
            src[t + 2, at, :] = stack[1, rr, cols]
        return carry

    for k, pair in enumerate(loads):
        for load in pair:
            load.wait()
        lax.fori_loop(k * TILES // PARTS, (k + 1) * TILES // PARTS, prepare, 0, unroll=UNROLL)

    spans = range(BASE, BASE + ROWS, 8)

    def step(t, wests):
        right = jnp.minimum(t + 1, WT - 1)
        easts = []
        for a, west in zip(spans, wests):
            at = pl.ds(a, 8)
            mid, f, east = flux(u0, coef, src, t, right, a, 8, west)
            d = rate[t, at, :] * f
            d1[t, at, :] = d
            fst[t, at, :] = mid + d
            easts.append(east)
        return tuple(easts)

    first_west = tuple(east_of(u0, 0, 0, a, 8) for a in spans)
    lax.fori_loop(0, WT, step, first_west, unroll=UNROLL)

    top = BASE + ROWS
    odd = place[4] == 1

    def send(at, row, up, low):
        msg_a[row, at] = jnp.where(odd, low, up)
        msg_b[row, at] = jnp.where(odd, up, low)

    for t in range(WT):
        at = pl.ds(t * LANES, LANES)
        send(at, slice(0, 2), u0[t, top - 2 : top, :], u0[t, BASE : BASE + 2, :])
        send(at, slice(2, 4), fst[t, top - 3 : top - 1, :], fst[t, BASE + 1 : BASE + 3, :])
    blank = jnp.zeros((1, LANES), F32)
    for k in range(16):
        at = pl.ds(WCOLS + (k % 4) * LANES, LANES)
        row = slice(k // 4, k // 4 + 1)
        if k < 14:
            up = both(k // 2, slice(ROWS - 1, ROWS))[k % 2]
            send(at, row, up, both(k // 2, slice(0, 1))[k % 2])
        else:
            send(at, row, blank, blank)


def second_step(fst, coef, src, rate, target, d2, mis, w, spans):
    def step(t, wests):
        easts = []
        for a, west in zip(spans, wests):
            at = pl.ds(a, 8)
            mid, f, east = flux(fst, coef, src, t, t + 1, a, 8, west)
            rt = rate[t, at, :]
            d = rt * f
            d2[t, at, :] = d
            m = (mid + d) - target[t, at, :]
            mis[t, at, :] = m
            w[t, at, :] = m * rt
            easts.append(east)
        return tuple(easts)

    return step, tuple(east_of(fst, 0, 1, a, 8) for a in spans)


def weigh_outlets(found, count, mis, w, inner):
    lane = lax.broadcasted_iota(jnp.int32, (1, LANES), 1)

    def weigh(i, carry):
        code = found[i]
        row, col = code >> 16, (code >> 6) & 127
        within = (row >= INNER[0]) & (row < INNER[-1] + 8)
        at = pl.ds(row, 1)
        tile = col >> 1

        @pl.when(within if inner else jnp.logical_not(within))
        def _():
            hit = lane == (col & 1) * NZ + (code & (NZ - 1))
            factor = jnp.where(hit, 1.0 + OUTLET_W, 1.0)
            mis[tile, at, :] = mis[tile, at, :] * factor
            w[tile, at, :] = w[tile, at, :] * factor

        return carry

    lax.fori_loop(0, count[0], weigh, 0)


def adjoint_step(coef, rate, mis, w, grad, w1, spans):
    def back(t, carry):
        for a in spans:
            at = pl.ds(a, 8)
            g = mis[t, at, :] + flux_back(w, coef, t, t - 1, t + 1, a, 8)
            grad[t, at, :] = g
            w1[t, at, :] = g * rate[t, at, :]
        return carry

    return back


def middle(found, count, x_a, x_b, y_a, y_b, t_h, fst, rate,
           cn_in, cs_in, ce_in, cw_in, cu_in, cd_in, cc_in, src_in,
           cn, cs, ce, cw, cu, cd, cc, src, target, kd_edge, d2, mis, w, grad, w1,
           tgt, halo, sem):
    load = pltpu.make_async_copy(t_h, tgt, sem)
    load.start()
    coef = (cn, cs, ce, cw, cu, cd, cc)
    place = places()
    odd = place[4] == 1
    own = pl.ds(BASE, ROWS)

    for parity, y_low, y_high in ((True, y_a, y_b), (False, y_b, y_a)):

        @pl.when(odd if parity else jnp.logical_not(odd))
        def _():
            for f in range(7):
                for t in range(TILES):
                    at = pl.ds(t * LANES, LANES)
                    halo[f, t, 6:8, :] = y_low[f, :, at]
                    halo[f, t, 8:10, :] = y_high[f, :, at]

    def edges(t, carry):
        for a, to in ((0, slice(0, BASE)), (8, slice(BASE + ROWS, WR))):
            at = pl.ds(a, 8)
            values = coefficients(*[halo[f, t, at, :] for f in (1, 2, 3, 5)])
            for ref, val in zip(coef, values):
                ref[t + 2, to, :] = val
            src[t + 2, to, :] = halo[4, t, at, :]
            target[t + 2, to, :] = halo[6, t, at, :]
            kd_edge[t + 2, at, :] = halo[0, t, at, :]
        return carry

    lax.fori_loop(0, TILES, edges, 0, unroll=4)
    load.wait()

    def targets(t, carry):
        at = pl.ds(pl.multiple_of(t * LANES, LANES), LANES)
        target[t + 2, own, :] = tgt[:, at]
        return carry

    lax.fori_loop(0, TILES, targets, 0, unroll=2)
    odd_x = place[5] == 1
    target[1, own, :] = jnp.where(odd_x, x_a[6], x_b[6])
    target[WT - 2, own, :] = jnp.where(odd_x, x_b[6], x_a[6])

    step, start = second_step(fst, coef, src, rate, target, d2, mis, w, INNER)
    lax.fori_loop(1, WT - 1, step, start, unroll=UNROLL)
    weigh_outlets(found, count, mis, w, True)
    back = adjoint_step(coef, rate, mis, w, grad, w1, BACK)
    lax.fori_loop(1, WT - 1, back, 0, unroll=UNROLL)


def second_half(found, count, msg_a, msg_b, kd_h, power, kd_edge_in,
                u0_in, fst_in, d1_in, rate_in, cn_in, cs_in, ce_in, cw_in, cu_in, cd_in, cc_in, src_in,
                 target_in, d2_in, mis_in, w_in, grad_in, w1_in,
                kd_out_h, start_out_h,
                u0, fst, d1, rate, cn, cs, ce, cw, cu, cd, cc, src, target, d2, mis, w, grad, w1,
                kd, kd_out, start_out, halo, sems):
    load = pltpu.make_async_copy(kd_h, kd, sems.at[0, 0])
    load.start()
    coef = (cn, cs, ce, cw, cu, cd, cc)
    low8, high8 = slice(0, BASE), slice(BASE + ROWS, WR)
    top = BASE + ROWS
    place = places()
    odd = place[4] == 1

    def arrived(row, at):
        one, two = msg_a[row, at], msg_b[row, at]
        return jnp.where(odd, one, two), jnp.where(odd, two, one)

    for t in range(WT):
        at = pl.ds(t * LANES, LANES)
        low, high = arrived(slice(0, 4), at)
        u0[t, 6:8, :] = low[0:2]
        fst[t, 5:7, :] = low[2:4]
        u0[t, top : top + 2, :] = high[0:2]
        fst[t, top + 1 : top + 3, :] = high[2:4]

    for f in range(7):
        for n in range(4):
            halo[f, n] = jnp.zeros((16, LANES), F32)
        for side, n in ((0, 1), (1, 2)):
            k = 2 * f + side
            low, high = arrived(slice(k // 4, k // 4 + 1), pl.ds(WCOLS + (k % 4) * LANES, LANES))
            halo[f, n, 7:8, :] = low
            halo[f, n, 8:9, :] = high
    for n, t in enumerate((0, 1, WT - 2, WT - 1)):
        for a, to in ((0, low8), (8, high8)):
            at = pl.ds(a, 8)
            values = coefficients(*[halo[f, n, at, :] for f in (1, 2, 3, 5)])
            for ref, val in zip(coef, values):
                ref[t, to, :] = val
            src[t, to, :] = halo[4, n, at, :]
            target[t, to, :] = halo[6, n, at, :]
            rate[t, to, :] = rate_of(halo[0, n, at, :], sorb(u0[t, to, :]))

    def edges(t, carry):
        for a, to in ((0, low8), (8, high8)):
            rate[t, to, :] = rate_of(kd_edge_in[t, pl.ds(a, 8), :], sorb(u0[t, to, :]))
        return carry

    lax.fori_loop(2, WT - 2, edges, 0, unroll=8)

    zero8 = jnp.zeros((WT, BASE, LANES), F32)
    edge_rows = (low8, high8)

    @pl.when(place[0] == 0)
    def _():
        for to in edge_rows:
            rate[0:2, to, :] = zero8[:2]
            u0[0:2, to, :] = zero8[:2]

    @pl.when(place[1] == 0)
    def _():
        for to in edge_rows:
            rate[WT - 2 : WT, to, :] = zero8[:2]
            u0[WT - 2 : WT, to, :] = zero8[:2]

    @pl.when(place[2] == 0)
    def _():
        rate[:, low8, :] = zero8
        u0[:, low8, :] = zero8
        fst[:, low8, :] = zero8

    @pl.when(place[3] == 0)
    def _():
        rate[:, high8, :] = zero8
        u0[:, high8, :] = zero8
        fst[:, high8, :] = zero8

    edge_spans = ((BASE - 4, BASE - 1), (top - 4, top - 1))

    def edge_step(t, wests):
        right = jnp.minimum(t + 1, WT - 1)
        easts = []
        for (a, r0), west in zip(edge_spans, wests):
            at = pl.ds(a, 8)
            row = lax.broadcasted_iota(jnp.int32, (8, LANES), 0) + a
            new = (row == r0) | (row == r0 + 1)
            mid, f, east = flux(u0, coef, src, t, right, a, 8, west)
            d = rate[t, at, :] * f
            d1[t, at, :] = jnp.where(new, d, d1[t, at, :])
            fst[t, at, :] = jnp.where(new, mid + d, fst[t, at, :])
            easts.append(east)
        return tuple(easts)

    first_west = tuple(east_of(u0, 0, 0, a, 8) for a, _ in edge_spans)
    lax.fori_loop(0, WT, edge_step, first_west, unroll=12)

    spans = range(BASE - 4, BASE + ROWS + 4, 8)
    outer = [a for a in spans if a not in INNER]
    step, start = second_step(fst, coef, src, rate, target, d2, mis, w, outer)
    lax.fori_loop(1, WT - 1, step, start, unroll=9)

    weigh_outlets(found, count, mis, w, False)
    back = adjoint_step(coef, rate, mis, w, grad, w1, [a for a in spans if a not in BACK])
    lax.fori_loop(1, WT - 1, back, 0, unroll=UNROLL)
    load.wait()

    def last(t, carry):
        cols = pl.ds(pl.multiple_of(t * LANES, LANES), LANES)
        tw = t + 2
        for r in range(0, ROWS, 8):
            a = BASE + r
            at, rr = pl.ds(a, 8), pl.ds(r, 8)
            g = grad[tw, at, :]
            start = g + flux_back(w1, coef, tw, tw - 1, tw + 1, a, 8)
            both = mis[tw, at, :] * d2[tw, at, :] + g * d1[tw, at, :]
            kdg = (both * rate[tw, at, :]) * (power[t, rr, :] * (-BULK / STEP))
            kd_out[rr, cols] = kdg
            start_out[rr, cols] = start + kdg * kd[rr, cols] * (FREUND - 1.0) / u0[tw, at, :]
        return carry

    parts = PARTS
    stores = []
    for k in range(parts):
        lax.fori_loop(k * TILES // parts, (k + 1) * TILES // parts, last, 0, unroll=UNROLL)
        cols = pl.ds(k * COLS // parts, COLS // parts)
        for a, b, n in ((kd_out, kd_out_h, 2), (start_out, start_out_h, 3)):
            stores.append(pltpu.make_async_copy(a.at[:, cols], b.at[:, cols], sems.at[n, k]))
            stores[-1].start()
    for store in stores:
        store.wait()


def params(mib):
    return pltpu.CompilerParams(vmem_limit_bytes=mib * MIB)


def swap(a, b, axis):
    n = lax.axis_size(axis)

    def pairs(first):
        return [(i, j) for k in range(first, n - 1, 2) for i, j in ((k, k + 1), (k + 1, k))]

    return lax.ppermute(a, axis, pairs(0)), lax.ppermute(b, axis, pairs(1))


def per_device(checkpoint, sorption_kd, velocity, source, target, cell_type, outlets):
    n_gx = lax.axis_size("gx")
    gx, gy = lax.axis_index("gx"), lax.axis_index("gy")
    lines = pl.pallas_call(
        pack_lines,
        out_shape=jax.ShapeDtypeStruct((n_gx, checkpoint.shape[1], WCOLS), F32),
        in_specs=[HB],
        out_specs=HB,
        scratch_shapes=[
            pltpu.VMEM((n_gx, checkpoint.shape[1], WCOLS), F32),
            pltpu.SemaphoreType.DMA((n_gx, 2)),
            pltpu.SemaphoreType.DMA((n_gx,)),
        ],
        compiler_params=params(60),
        name="pack_lines",
    )(checkpoint)
    arrived = lax.all_to_all(lines, "gx", split_axis=0, concat_axis=0, tiled=True)

    side = jax.ShapeDtypeStruct((10, ROWS, LANES), F32)
    line = jax.ShapeDtypeStruct((7, 2, COLS), F32)
    row = (outlets >> 16) - gy * ROWS + BASE
    col = ((outlets >> 6) & 1023) - gx * (COLS // NZ) + 4
    inside = (row >= BASE - 2) & (row < BASE + ROWS + 2) & (col >= 2) & (col < 70)
    codes = jnp.where(inside, (row << 16) + (col << 6) + (outlets & (NZ - 1)), -1)
    code_rows = codes.reshape(-1, LANES)
    rows = ROWS // PACK_BLOCKS
    flat = pl.BlockSpec((rows, COLS), lambda i: (i, 0))
    two = 2 * LANES

    def block_specs(lead, *blocks):
        return [
            pl.BlockSpec(lead + shape, lambda i, at=at: (0,) * len(lead) + at) for shape, at in blocks
        ]

    sides = ((ROWS, two), (0, 0)), ((ROWS, two), (0, TILES // 2 - 1))
    ends = ((8, COLS), (0, 0)), ((8, COLS), (ROWS // 8 - 1, 0))
    fields = (sorption_kd, velocity, source, cell_type, target)
    twice = [f for f in fields for _ in range(2)]

    def specs(blocks):
        return [b for f in fields for b in block_specs((3,) if f.ndim == 3 else (), *blocks)]

    whole = lambda a: pl.BlockSpec(a.shape, lambda i: (0, 0, 0))
    side_a, side_b = pl.pallas_call(
        pack_sides,
        grid=(1,),
        out_shape=[side, side],
        in_specs=specs(sides),
        out_specs=[whole(side), whole(side)],
        compiler_params=params(60),
        name="pack_sides",
    )(*twice)
    stack, line_a, line_b, found, count = pl.pallas_call(
        stack_fields,
        grid=(PACK_BLOCKS,),
        out_shape=[
            jax.ShapeDtypeStruct((STACK, ROWS, COLS), F32), line, line,
            jax.ShapeDtypeStruct((outlets.shape[0],), jnp.int32),
            jax.ShapeDtypeStruct((1,), jnp.int32),
        ],
        in_specs=[HB, SM, pl.BlockSpec(code_rows.shape, lambda i: (0, 0)), flat, flat, flat]
        + specs(ends),
        out_specs=[
            pl.BlockSpec((3, rows, COLS), lambda i: (0, i, 0)), whole(line), whole(line), SM, SM,
        ],
        compiler_params=params(60),
        name="stack_fields",
    )(side_a, codes, code_rows, sorption_kd, source, cell_type, *twice)
    x_a, x_b = swap(side_a, side_b, "gx")
    y_a, y_b = swap(line_a, line_b, "gy")

    message = jax.ShapeDtypeStruct((4, MCOLS), F32)
    power = jax.ShapeDtypeStruct((TILES, ROWS, LANES), F32)
    u0, fst, d1, rate, power, *rest = pl.pallas_call(
        first_half,
        out_shape=[window()] * 4 + [power] + [window()] * 8 + [message] * 2,
        in_specs=[VM] * 3 + [HB] * 2,
        out_specs=[VM] * 15,
        scratch_shapes=[*[pltpu.VMEM((3, ROWS, COLS), F32)] * 2, pltpu.SemaphoreType.DMA((2 * PARTS,))],
        compiler_params=params(FIRST_MIB),
        name="first_half",
    )(arrived, x_a, x_b, velocity, stack)
    coefs, (msg_a, msg_b) = rest[:8], rest[8:]
    got_a, got_b = swap(msg_a, msg_b, "gy")

    edge_kd = jax.ShapeDtypeStruct((WT, 16, LANES), F32)
    *coefs, aim, kd_edge, d2, mis, w, grad, w1 = pl.pallas_call(
        middle,
        out_shape=[window()] * 9 + [edge_kd] + [window()] * 5,
        in_specs=[SM] * 2 + [VM] * 4 + [HB] + [VM] * 10,
        out_specs=[VM] * 15,
        input_output_aliases={9 + k: k for k in range(8)},
        scratch_shapes=[
            pltpu.VMEM((ROWS, COLS), F32),
            pltpu.VMEM((7, TILES, 16, LANES), F32),
            pltpu.SemaphoreType.DMA,
        ],
        compiler_params=params(8),
        name="middle",
    )(found, count, x_a, x_b, y_a, y_b, target, fst, rate, *coefs)

    kept = (u0, fst, d1, rate, *coefs, aim, d2, mis, w, grad, w1)
    plane = jax.ShapeDtypeStruct((ROWS, COLS), F32)
    outs = pl.pallas_call(
        second_half,
        out_shape=[plane, plane] + [window()] * 18,
        in_specs=[SM] * 2 + [VM] * 2 + [HB] + [VM] * 20,
        out_specs=[HB] * 2 + [VM] * 18,
        input_output_aliases={7 + k: 2 + k for k in range(18)},
        scratch_shapes=[
            *[pltpu.VMEM((ROWS, COLS), F32)] * 3,
            pltpu.VMEM((7, 4, 16, LANES), F32),
            pltpu.SemaphoreType.DMA((4, 4)),
        ],
        compiler_params=params(12),
        name="second_half",
    )(found, count, got_a, got_b, sorption_kd, power, kd_edge, *kept)
    return outs[0], outs[1]


def solution(mesh):
    return jax.shard_map(
        per_device,
        mesh=mesh,
        in_specs=(
            P("gy", "gx", None),
            P("gy", "gx"),
            P(None, "gy", "gx"),
            P("gy", "gx"),
            P("gy", "gx"),
            P("gy", "gx"),
            P(),
        ),
        out_specs=(P("gy", "gx"), P("gy", "gx")),
        check_vma=False,
    )
```

```python
import jax
import jax.numpy as jnp
from jax import lax
from jax.experimental import pallas as pl
from jax.experimental.pallas import tpu as pltpu
from jax.sharding import PartitionSpec as P

NZ = 64
BULK = 4.0
FREUND = 0.7
DISP = 0.1
DRAIN = 0.5
STEP = 0.4
OUTLET_W = 4.0

LANES = 128
ROWS = 64
TILES = 32
WT = TILES + 4
WR = 80
BASE = 8
INNER = range(BASE + 4, BASE + ROWS - 8, 8)
BACK = range(INNER[0] + 8, INNER[-1], 8)
COLS = TILES * LANES
WCOLS = WT * LANES
MCOLS = WCOLS + 4 * LANES
F32 = jnp.float32
MIB = 1 << 20
FIRST_MIB = 27
STACK = 6
UNROLL = 8
PACK_BLOCKS = 4
PARTS = 4


def places():
    gx, gy = lax.axis_index("gx"), lax.axis_index("gy")
    return (
        gx, lax.axis_size("gx") - 1 - gx, gy, lax.axis_size("gy") - 1 - gy,
        lax.rem(gy, 2), lax.rem(gx, 2),
    )


VM = pl.BlockSpec(memory_space=pltpu.VMEM)
SM = pl.BlockSpec(memory_space=pltpu.SMEM)
HB = pl.BlockSpec(memory_space=pltpu.HBM)


def window(dtype=F32):
    return jax.ShapeDtypeStruct((WT, WR, LANES), dtype)


def lane_iota(rows):
    return lax.broadcasted_iota(jnp.int32, (rows, LANES), 1)


def pack_lines(src, out, held, arrived, sent):
    n = out.shape[0]
    loads, stores = [], []
    for i in range(n):
        low = i * COLS - 2 * LANES
        high = low + WCOLS
        a, b = max(low, 0), min(high, n * COLS)
        at = a - low
        pieces = [(a, b, at)]
        if low < 0:
            pieces.append((0, 2 * LANES, 0))
        if high > n * COLS:
            pieces.append((n * COLS - 2 * LANES, n * COLS, WCOLS - 2 * LANES))
        loads.append([
            pltpu.make_async_copy(
                src.at[0, :, a:b], held.at[i, :, at : at + b - a], arrived.at[i, k]
            )
            for k, (a, b, at) in enumerate(pieces)
        ])
        stores.append(pltpu.make_async_copy(held.at[i], out.at[i], sent.at[i]))
    for group in loads:
        for c in group:
            c.start()
    for group, store in zip(loads, stores):
        for c in group:
            c.wait()
        store.start()
    for store in stores:
        store.wait()


def all_fields(kd, v, s, c, t, at):
    kind = c[at]
    return (
        kd[at], *[v[(d, *at)] for d in range(3)],
        jnp.where(kind == 1, s[at], 0.0),
        jnp.where(kind == 2, DRAIN, 0.0).astype(F32),
        t[at],
    )


def pack_sides(kdl, kdr, vl, vr, sl, sr, cl, cr, tl, tr, side_a, side_b):
    odd = places()[5] == 1
    lo = lane_iota(ROWS) < NZ

    def layers(refs, near, far, low_side):
        def tile(k):
            return all_fields(*refs, (slice(None), slice(k * LANES, (k + 1) * LANES)))
        part = tile(far)
        merged = []
        for p in range(3):
            first, second = part[2 * p], part[2 * p + 1]
            if low_side:
                second = pltpu.roll(second, NZ, 1)
            else:
                first = pltpu.roll(first, NZ, 1)
            merged.append(jnp.where(lo, first, second))
        return list(tile(near)) + merged

    low_side = layers((kdl, vl, sl, cl, tl), 0, 1, True)
    high_side = layers((kdr, vr, sr, cr, tr), 1, 0, False)
    for f, (low, high) in enumerate(zip(low_side, high_side)):
        side_a[f] = jnp.where(odd, low, high)
        side_b[f] = jnp.where(odd, high, low)


def stack_fields(side, codes, code_rows, kd, s, c, kdt, kdb, vt, vb, st, sb, ct, cb, tt, tb,
                 stack, line_a, line_b, found, count):
    stack[0] = kd[...]
    stack[1] = jnp.where(c[...] == 1, s[...], 0.0)
    stack[2] = jnp.where(c[...] == 2, DRAIN, 0.0).astype(F32)

    @pl.when(pl.program_id(0) == 0)
    def _():
        odd = places()[4] == 1
        low_line = all_fields(kdt, vt, st, ct, tt, (slice(0, 2), slice(None)))
        high_line = all_fields(kdb, vb, sb, cb, tb, (slice(6, 8), slice(None)))
        for f, (low, high) in enumerate(zip(low_line, high_line)):
            line_a[f] = jnp.where(odd, low, high)
            line_b[f] = jnp.where(odd, high, low)


    @pl.when(pl.program_id(0) == 0)
    def _():
        count[0] = 0

    unroll = 32
    share = code_rows.shape[0] // PACK_BLOCKS
    for k in range(share):
        row = pl.program_id(0) * share + k

        @pl.when(jnp.max(code_rows[pl.ds(row, 1), :].astype(F32)) >= 0.0)
        def _():
            def compact(i, n):
                values = [codes[row * LANES + i * unroll + j] for j in range(unroll)]
                for value in values:
                    found[n] = value
                    n = n + 1 + (value >> 31)
                return n

            count[0] = lax.fori_loop(0, LANES // unroll, compact, count[0])


def coefficients(v0, v1, v2, drain):
    z = lax.broadcasted_iota(jnp.int32, v0.shape, v0.ndim - 1) & (NZ - 1)
    north = DISP - jnp.minimum(v0, 0.0)
    south = DISP + jnp.maximum(v0, 0.0)
    east = DISP - jnp.minimum(v1, 0.0)
    west = DISP + jnp.maximum(v1, 0.0)
    up = jnp.where(z == NZ - 1, 0.0, DISP - jnp.minimum(v2, 0.0))
    down = jnp.where(z == 0, 0.0, DISP + jnp.maximum(v2, 0.0))
    centre = ((north + south) + (east + west)) + ((up + down) + drain)
    return north, south, east, west, up, down, centre


def east_of(u, t, right, a, rows):
    here = pl.ds(a, rows)
    lo = lane_iota(rows) < NZ
    return pltpu.roll(jnp.where(lo, u[right, here, :], u[t, here, :]), NZ, 1)


def flux(u, coef, src, t, right, a, rows, west):
    cn, cs, ce, cw, cu, cd, cc = coef
    here = pl.ds(a, rows)
    mid = u[t, here, :]
    north = u[t, pl.ds(a + 1, rows), :]
    south = u[t, pl.ds(a - 1, rows), :]
    east = east_of(u, t, right, a, rows)
    upper = pltpu.roll(mid, LANES - 1, 1)
    lower = pltpu.roll(mid, 1, 1)
    plane = cn[t, here, :] * north + cs[t, here, :] * south
    plane = plane + (ce[t, here, :] * east + cw[t, here, :] * west)
    plane = plane + (cu[t, here, :] * upper + cd[t, here, :] * lower)
    return mid, plane + (src[t, here, :] - cc[t, here, :] * mid), east


def flux_back(w, coef, t, left, right, a, rows):
    cn, cs, ce, cw, cu, cd, cc = coef
    here = pl.ds(a, rows)
    above, below = pl.ds(a + 1, rows), pl.ds(a - 1, rows)
    lo = lane_iota(rows) < NZ
    mid = w[t, here, :]
    w_right, w_left = w[right, here, :], w[left, here, :]
    from_low = cw[right, here, :] * w_right + ce[t, here, :] * mid
    from_high = cw[t, here, :] * mid + ce[left, here, :] * w_left
    total = pltpu.roll(jnp.where(lo, from_low, from_high), NZ, 1)
    total = total + (cs[t, above, :] * w[t, above, :] + cn[t, below, :] * w[t, below, :])
    total = total + pltpu.roll(cd[t, here, :] * mid, LANES - 1, 1)
    total = total + pltpu.roll(cu[t, here, :] * mid, 1, 1)
    return total - cc[t, here, :] * mid


def sorb(u):
    return jnp.exp((FREUND - 1.0) * jnp.log(u))


def rate_of(kd, power):
    return STEP / (1.0 + BULK * kd * power)


def first_half(lines, x_a, x_b, v_h, stack_h,
               u0, fst, d1, rate, power, cn, cs, ce, cw, cu, cd, cc, src, msg_a, msg_b,
               v, stack, sems):
    loads = []
    for k in range(PARTS):
        cols = pl.ds(k * COLS // PARTS, COLS // PARTS)
        loads.append([
            pltpu.make_async_copy(stack_h.at[0:3, :, cols], stack.at[:, :, cols], sems.at[2 * k]),
            pltpu.make_async_copy(v_h.at[:, :, cols], v.at[:, :, cols], sems.at[2 * k + 1]),
        ])
    for pair in loads:
        for load in pair:
            load.start()
    coef = (cn, cs, ce, cw, cu, cd, cc)
    own = pl.ds(BASE, ROWS)
    lines_of = lines.shape[1]
    for k in range(lines.shape[0]):
        for t in range(WT):
            u0[t, BASE + lines_of * k : BASE + lines_of * (k + 1), :] = lines[
                k, :, t * LANES : (t + 1) * LANES
            ]
    lo = lane_iota(ROWS) < NZ

    place = places()
    odd_x = place[5] == 1

    def both(f, rows=slice(None)):
        one, two = x_a[f, rows], x_b[f, rows]
        return jnp.where(odd_x, one, two), jnp.where(odd_x, two, one)

    low_x, high_x = zip(*[both(f) for f in range(6)])
    low_3, high_3 = zip(*[both(f) for f in range(7, 10)])

    def third(parts, f, high):
        part = parts[f // 2]
        if high:
            return jnp.where(lo, 0.0, part if f % 2 else pltpu.roll(part, NZ, 1))
        return jnp.where(lo, pltpu.roll(part, NZ, 1) if f % 2 else part, 0.0)

    for tile, fields in (
        (0, [third(low_3, f, True) for f in range(6)]),
        (1, low_x),
        (WT - 2, high_x),
        (WT - 1, [third(high_3, f, False) for f in range(6)]),
    ):
        for ref, val in zip(coef, coefficients(*fields[1:4], fields[5])):
            ref[tile, own, :] = val
        src[tile, own, :] = fields[4]
        rate[tile, own, :] = rate_of(fields[0], sorb(u0[tile, own, :]))

    @pl.when(place[0] == 0)
    def _():
        for ref in (u0, rate):
            ref[0:2, own, :] = jnp.zeros((2, ROWS, LANES), F32)

    @pl.when(place[1] == 0)
    def _():
        for ref in (u0, rate):
            ref[WT - 2 : WT, own, :] = jnp.zeros((2, ROWS, LANES), F32)

    def prepare(t, carry):
        cols = pl.ds(pl.multiple_of(t * LANES, LANES), LANES)
        for r in range(0, ROWS, 8):
            rr, at = pl.ds(r, 8), pl.ds(BASE + r, 8)
            p = sorb(u0[t + 2, at, :])
            power[t, rr, :] = p
            rate[t + 2, at, :] = rate_of(stack[0, rr, cols], p)
            values = coefficients(
                v[0, rr, cols], v[1, rr, cols], v[2, rr, cols], stack[2, rr, cols]
            )
            for ref, val in zip(coef, values):
                ref[t + 2, at, :] = val
            src[t + 2, at, :] = stack[1, rr, cols]
        return carry

    for k, pair in enumerate(loads):
        for load in pair:
            load.wait()
        lax.fori_loop(k * TILES // PARTS, (k + 1) * TILES // PARTS, prepare, 0, unroll=UNROLL)

    spans = range(BASE, BASE + ROWS, 8)

    def step(t, wests):
        right = jnp.minimum(t + 1, WT - 1)
        easts = []
        for a, west in zip(spans, wests):
            at = pl.ds(a, 8)
            mid, f, east = flux(u0, coef, src, t, right, a, 8, west)
            d = rate[t, at, :] * f
            d1[t, at, :] = d
            fst[t, at, :] = mid + d
            easts.append(east)
        return tuple(easts)

    first_west = tuple(east_of(u0, 0, 0, a, 8) for a in spans)
    lax.fori_loop(0, WT, step, first_west, unroll=UNROLL)

    top = BASE + ROWS
    odd = place[4] == 1

    def send(at, row, up, low):
        msg_a[row, at] = jnp.where(odd, low, up)
        msg_b[row, at] = jnp.where(odd, up, low)

    for t in range(WT):
        at = pl.ds(t * LANES, LANES)
        send(at, slice(0, 2), u0[t, top - 2 : top, :], u0[t, BASE : BASE + 2, :])
        send(at, slice(2, 4), fst[t, top - 3 : top - 1, :], fst[t, BASE + 1 : BASE + 3, :])
    blank = jnp.zeros((1, LANES), F32)
    for k in range(16):
        at = pl.ds(WCOLS + (k % 4) * LANES, LANES)
        row = slice(k // 4, k // 4 + 1)
        if k < 14:
            up = both(k // 2, slice(ROWS - 1, ROWS))[k % 2]
            send(at, row, up, both(k // 2, slice(0, 1))[k % 2])
        else:
            send(at, row, blank, blank)


def second_step(fst, coef, src, rate, target, d2, mis, w, spans):
    def step(t, wests):
        easts = []
        for a, west in zip(spans, wests):
            at = pl.ds(a, 8)
            mid, f, east = flux(fst, coef, src, t, t + 1, a, 8, west)
            rt = rate[t, at, :]
            d = rt * f
            d2[t, at, :] = d
            m = (mid + d) - target[t, at, :]
            mis[t, at, :] = m
            w[t, at, :] = m * rt
            easts.append(east)
        return tuple(easts)

    return step, tuple(east_of(fst, 0, 1, a, 8) for a in spans)


def weigh_outlets(found, count, mis, w, inner):
    lane = lax.broadcasted_iota(jnp.int32, (1, LANES), 1)

    def weigh(i, carry):
        code = found[i]
        row, col = code >> 16, (code >> 6) & 127
        within = (row >= INNER[0]) & (row < INNER[-1] + 8)
        at = pl.ds(row, 1)
        tile = col >> 1

        @pl.when(within if inner else jnp.logical_not(within))
        def _():
            hit = lane == (col & 1) * NZ + (code & (NZ - 1))
            factor = jnp.where(hit, 1.0 + OUTLET_W, 1.0)
            mis[tile, at, :] = mis[tile, at, :] * factor
            w[tile, at, :] = w[tile, at, :] * factor

        return carry

    lax.fori_loop(0, count[0], weigh, 0)


def adjoint_step(coef, rate, mis, w, grad, w1, spans):
    def back(t, carry):
        for a in spans:
            at = pl.ds(a, 8)
            g = mis[t, at, :] + flux_back(w, coef, t, t - 1, t + 1, a, 8)
            grad[t, at, :] = g
            w1[t, at, :] = g * rate[t, at, :]
        return carry

    return back


def middle(found, count, x_a, x_b, y_a, y_b, t_h, fst, rate,
           cn_in, cs_in, ce_in, cw_in, cu_in, cd_in, cc_in, src_in,
           cn, cs, ce, cw, cu, cd, cc, src, target, kd_edge, d2, mis, w, grad, w1,
           tgt, halo, sem):
    load = pltpu.make_async_copy(t_h, tgt, sem)
    load.start()
    coef = (cn, cs, ce, cw, cu, cd, cc)
    place = places()
    odd = place[4] == 1
    own = pl.ds(BASE, ROWS)

    for parity, y_low, y_high in ((True, y_a, y_b), (False, y_b, y_a)):

        @pl.when(odd if parity else jnp.logical_not(odd))
        def _():
            for f in range(7):
                for t in range(TILES):
                    at = pl.ds(t * LANES, LANES)
                    halo[f, t, 6:8, :] = y_low[f, :, at]
                    halo[f, t, 8:10, :] = y_high[f, :, at]

    def edges(t, carry):
        for a, to in ((0, slice(0, BASE)), (8, slice(BASE + ROWS, WR))):
            at = pl.ds(a, 8)
            values = coefficients(*[halo[f, t, at, :] for f in (1, 2, 3, 5)])
            for ref, val in zip(coef, values):
                ref[t + 2, to, :] = val
            src[t + 2, to, :] = halo[4, t, at, :]
            target[t + 2, to, :] = halo[6, t, at, :]
            kd_edge[t + 2, at, :] = halo[0, t, at, :]
        return carry

    lax.fori_loop(0, TILES, edges, 0, unroll=4)
    load.wait()

    def targets(t, carry):
        at = pl.ds(pl.multiple_of(t * LANES, LANES), LANES)
        target[t + 2, own, :] = tgt[:, at]
        return carry

    lax.fori_loop(0, TILES, targets, 0, unroll=2)
    odd_x = place[5] == 1
    target[1, own, :] = jnp.where(odd_x, x_a[6], x_b[6])
    target[WT - 2, own, :] = jnp.where(odd_x, x_b[6], x_a[6])

    step, start = second_step(fst, coef, src, rate, target, d2, mis, w, INNER)
    lax.fori_loop(1, WT - 1, step, start, unroll=UNROLL)
    weigh_outlets(found, count, mis, w, True)
    back = adjoint_step(coef, rate, mis, w, grad, w1, BACK)
    lax.fori_loop(1, WT - 1, back, 0, unroll=UNROLL)


def second_half(found, count, msg_a, msg_b, kd_h, power, kd_edge_in,
                u0_in, fst_in, d1_in, rate_in, cn_in, cs_in, ce_in, cw_in, cu_in, cd_in, cc_in, src_in,
                 target_in, d2_in, mis_in, w_in, grad_in, w1_in,
                kd_out_h, start_out_h,
                u0, fst, d1, rate, cn, cs, ce, cw, cu, cd, cc, src, target, d2, mis, w, grad, w1,
                kd, kd_out, start_out, halo, sems):
    load = pltpu.make_async_copy(kd_h, kd, sems.at[0, 0])
    load.start()
    coef = (cn, cs, ce, cw, cu, cd, cc)
    low8, high8 = slice(0, BASE), slice(BASE + ROWS, WR)
    top = BASE + ROWS
    place = places()
    odd = place[4] == 1

    def arrived(row, at):
        one, two = msg_a[row, at], msg_b[row, at]
        return jnp.where(odd, one, two), jnp.where(odd, two, one)

    for t in range(WT):
        at = pl.ds(t * LANES, LANES)
        low, high = arrived(slice(0, 4), at)
        u0[t, 6:8, :] = low[0:2]
        fst[t, 5:7, :] = low[2:4]
        u0[t, top : top + 2, :] = high[0:2]
        fst[t, top + 1 : top + 3, :] = high[2:4]

    for f in range(7):
        for n in range(4):
            halo[f, n] = jnp.zeros((16, LANES), F32)
        for side, n in ((0, 1), (1, 2)):
            k = 2 * f + side
            low, high = arrived(slice(k // 4, k // 4 + 1), pl.ds(WCOLS + (k % 4) * LANES, LANES))
            halo[f, n, 7:8, :] = low
            halo[f, n, 8:9, :] = high
    for n, t in enumerate((0, 1, WT - 2, WT - 1)):
        for a, to in ((0, low8), (8, high8)):
            at = pl.ds(a, 8)
            values = coefficients(*[halo[f, n, at, :] for f in (1, 2, 3, 5)])
            for ref, val in zip(coef, values):
                ref[t, to, :] = val
            src[t, to, :] = halo[4, n, at, :]
            target[t, to, :] = halo[6, n, at, :]
            rate[t, to, :] = rate_of(halo[0, n, at, :], sorb(u0[t, to, :]))

    def edges(t, carry):
        for a, to in ((0, low8), (8, high8)):
            rate[t, to, :] = rate_of(kd_edge_in[t, pl.ds(a, 8), :], sorb(u0[t, to, :]))
        return carry

    lax.fori_loop(2, WT - 2, edges, 0, unroll=8)

    zero8 = jnp.zeros((WT, BASE, LANES), F32)
    edge_rows = (low8, high8)

    @pl.when(place[0] == 0)
    def _():
        for to in edge_rows:
            rate[0:2, to, :] = zero8[:2]
            u0[0:2, to, :] = zero8[:2]

    @pl.when(place[1] == 0)
    def _():
        for to in edge_rows:
            rate[WT - 2 : WT, to, :] = zero8[:2]
            u0[WT - 2 : WT, to, :] = zero8[:2]

    @pl.when(place[2] == 0)
    def _():
        rate[:, low8, :] = zero8
        u0[:, low8, :] = zero8
        fst[:, low8, :] = zero8

    @pl.when(place[3] == 0)
    def _():
        rate[:, high8, :] = zero8
        u0[:, high8, :] = zero8
        fst[:, high8, :] = zero8

    edge_spans = ((BASE - 4, BASE - 1), (top - 4, top - 1))

    def edge_step(t, wests):
        right = jnp.minimum(t + 1, WT - 1)
        easts = []
        for (a, r0), west in zip(edge_spans, wests):
            at = pl.ds(a, 8)
            row = lax.broadcasted_iota(jnp.int32, (8, LANES), 0) + a
            new = (row == r0) | (row == r0 + 1)
            mid, f, east = flux(u0, coef, src, t, right, a, 8, west)
            d = rate[t, at, :] * f
            d1[t, at, :] = jnp.where(new, d, d1[t, at, :])
            fst[t, at, :] = jnp.where(new, mid + d, fst[t, at, :])
            easts.append(east)
        return tuple(easts)

    first_west = tuple(east_of(u0, 0, 0, a, 8) for a, _ in edge_spans)
    lax.fori_loop(0, WT, edge_step, first_west, unroll=18)

    spans = range(BASE - 4, BASE + ROWS + 4, 8)
    outer = [a for a in spans if a not in INNER]
    step, start = second_step(fst, coef, src, rate, target, d2, mis, w, outer)
    lax.fori_loop(1, WT - 1, step, start, unroll=17)

    weigh_outlets(found, count, mis, w, False)
    back = adjoint_step(coef, rate, mis, w, grad, w1, [a for a in spans if a not in BACK])
    lax.fori_loop(1, WT - 1, back, 0, unroll=UNROLL)
    load.wait()

    def last(t, carry):
        cols = pl.ds(pl.multiple_of(t * LANES, LANES), LANES)
        tw = t + 2
        for r in range(0, ROWS, 8):
            a = BASE + r
            at, rr = pl.ds(a, 8), pl.ds(r, 8)
            g = grad[tw, at, :]
            start = g + flux_back(w1, coef, tw, tw - 1, tw + 1, a, 8)
            both = mis[tw, at, :] * d2[tw, at, :] + g * d1[tw, at, :]
            kdg = (both * rate[tw, at, :]) * (power[t, rr, :] * (-BULK / STEP))
            kd_out[rr, cols] = kdg
            start_out[rr, cols] = start + kdg * kd[rr, cols] * (FREUND - 1.0) / u0[tw, at, :]
        return carry

    parts = PARTS
    stores = []
    for k in range(parts):
        lax.fori_loop(k * TILES // parts, (k + 1) * TILES // parts, last, 0, unroll=UNROLL)
        cols = pl.ds(k * COLS // parts, COLS // parts)
        for a, b, n in ((kd_out, kd_out_h, 2), (start_out, start_out_h, 3)):
            stores.append(pltpu.make_async_copy(a.at[:, cols], b.at[:, cols], sems.at[n, k]))
            stores[-1].start()
    for store in stores:
        store.wait()


def params(mib):
    return pltpu.CompilerParams(vmem_limit_bytes=mib * MIB)


def swap(a, b, axis):
    n = lax.axis_size(axis)

    def pairs(first):
        return [(i, j) for k in range(first, n - 1, 2) for i, j in ((k, k + 1), (k + 1, k))]

    return lax.ppermute(a, axis, pairs(0)), lax.ppermute(b, axis, pairs(1))


def per_device(checkpoint, sorption_kd, velocity, source, target, cell_type, outlets):
    n_gx = lax.axis_size("gx")
    gx, gy = lax.axis_index("gx"), lax.axis_index("gy")
    lines = pl.pallas_call(
        pack_lines,
        out_shape=jax.ShapeDtypeStruct((n_gx, checkpoint.shape[1], WCOLS), F32),
        in_specs=[HB],
        out_specs=HB,
        scratch_shapes=[
            pltpu.VMEM((n_gx, checkpoint.shape[1], WCOLS), F32),
            pltpu.SemaphoreType.DMA((n_gx, 2)),
            pltpu.SemaphoreType.DMA((n_gx,)),
        ],
        compiler_params=params(60),
        name="pack_lines",
    )(checkpoint)
    arrived = lax.all_to_all(lines, "gx", split_axis=0, concat_axis=0, tiled=True)

    side = jax.ShapeDtypeStruct((10, ROWS, LANES), F32)
    line = jax.ShapeDtypeStruct((7, 2, COLS), F32)
    row = (outlets >> 16) - gy * ROWS + BASE
    col = ((outlets >> 6) & 1023) - gx * (COLS // NZ) + 4
    inside = (row >= BASE - 2) & (row < BASE + ROWS + 2) & (col >= 2) & (col < 70)
    codes = jnp.where(inside, (row << 16) + (col << 6) + (outlets & (NZ - 1)), -1)
    code_rows = codes.reshape(-1, LANES)
    rows = ROWS // PACK_BLOCKS
    flat = pl.BlockSpec((rows, COLS), lambda i: (i, 0))
    two = 2 * LANES

    def block_specs(lead, *blocks):
        return [
            pl.BlockSpec(lead + shape, lambda i, at=at: (0,) * len(lead) + at) for shape, at in blocks
        ]

    sides = ((ROWS, two), (0, 0)), ((ROWS, two), (0, TILES // 2 - 1))
    ends = ((8, COLS), (0, 0)), ((8, COLS), (ROWS // 8 - 1, 0))
    fields = (sorption_kd, velocity, source, cell_type, target)
    twice = [f for f in fields for _ in range(2)]

    def specs(blocks):
        return [b for f in fields for b in block_specs((3,) if f.ndim == 3 else (), *blocks)]

    whole = lambda a: pl.BlockSpec(a.shape, lambda i: (0, 0, 0))
    side_a, side_b = pl.pallas_call(
        pack_sides,
        grid=(1,),
        out_shape=[side, side],
        in_specs=specs(sides),
        out_specs=[whole(side), whole(side)],
        compiler_params=params(60),
        name="pack_sides",
    )(*twice)
    stack, line_a, line_b, found, count = pl.pallas_call(
        stack_fields,
        grid=(PACK_BLOCKS,),
        out_shape=[
            jax.ShapeDtypeStruct((STACK, ROWS, COLS), F32), line, line,
            jax.ShapeDtypeStruct((outlets.shape[0],), jnp.int32),
            jax.ShapeDtypeStruct((1,), jnp.int32),
        ],
        in_specs=[HB, SM, pl.BlockSpec(code_rows.shape, lambda i: (0, 0)), flat, flat, flat]
        + specs(ends),
        out_specs=[
            pl.BlockSpec((3, rows, COLS), lambda i: (0, i, 0)), whole(line), whole(line), SM, SM,
        ],
        compiler_params=params(60),
        name="stack_fields",
    )(side_a, codes, code_rows, sorption_kd, source, cell_type, *twice)
    x_a, x_b = swap(side_a, side_b, "gx")
    y_a, y_b = swap(line_a, line_b, "gy")

    message = jax.ShapeDtypeStruct((4, MCOLS), F32)
    power = jax.ShapeDtypeStruct((TILES, ROWS, LANES), F32)
    u0, fst, d1, rate, power, *rest = pl.pallas_call(
        first_half,
        out_shape=[window()] * 4 + [power] + [window()] * 8 + [message] * 2,
        in_specs=[VM] * 3 + [HB] * 2,
        out_specs=[VM] * 15,
        scratch_shapes=[*[pltpu.VMEM((3, ROWS, COLS), F32)] * 2, pltpu.SemaphoreType.DMA((2 * PARTS,))],
        compiler_params=params(FIRST_MIB),
        name="first_half",
    )(arrived, x_a, x_b, velocity, stack)
    coefs, (msg_a, msg_b) = rest[:8], rest[8:]
    got_a, got_b = swap(msg_a, msg_b, "gy")

    edge_kd = jax.ShapeDtypeStruct((WT, 16, LANES), F32)
    *coefs, aim, kd_edge, d2, mis, w, grad, w1 = pl.pallas_call(
        middle,
        out_shape=[window()] * 9 + [edge_kd] + [window()] * 5,
        in_specs=[SM] * 2 + [VM] * 4 + [HB] + [VM] * 10,
        out_specs=[VM] * 15,
        input_output_aliases={9 + k: k for k in range(8)},
        scratch_shapes=[
            pltpu.VMEM((ROWS, COLS), F32),
            pltpu.VMEM((7, TILES, 16, LANES), F32),
            pltpu.SemaphoreType.DMA,
        ],
        compiler_params=params(8),
        name="middle",
    )(found, count, x_a, x_b, y_a, y_b, target, fst, rate, *coefs)

    kept = (u0, fst, d1, rate, *coefs, aim, d2, mis, w, grad, w1)
    plane = jax.ShapeDtypeStruct((ROWS, COLS), F32)
    outs = pl.pallas_call(
        second_half,
        out_shape=[plane, plane] + [window()] * 18,
        in_specs=[SM] * 2 + [VM] * 2 + [HB] + [VM] * 20,
        out_specs=[HB] * 2 + [VM] * 18,
        input_output_aliases={7 + k: 2 + k for k in range(18)},
        scratch_shapes=[
            *[pltpu.VMEM((ROWS, COLS), F32)] * 3,
            pltpu.VMEM((7, 4, 16, LANES), F32),
            pltpu.SemaphoreType.DMA((4, 4)),
        ],
        compiler_params=params(12),
        name="second_half",
    )(found, count, got_a, got_b, sorption_kd, power, kd_edge, *kept)
    return outs[0], outs[1]


def solution(mesh):
    return jax.shard_map(
        per_device,
        mesh=mesh,
        in_specs=(
            P("gy", "gx", None),
            P("gy", "gx"),
            P(None, "gy", "gx"),
            P("gy", "gx"),
            P("gy", "gx"),
            P("gy", "gx"),
            P(),
        ),
        out_specs=(P("gy", "gx"), P("gy", "gx")),
        check_vma=False,
    )
```

```python
import jax
import jax.numpy as jnp
from jax import lax
from jax.experimental import pallas as pl
from jax.experimental.pallas import tpu as pltpu
from jax.sharding import PartitionSpec as P

NZ = 64
BULK = 4.0
FREUND = 0.7
DISP = 0.1
DRAIN = 0.5
STEP = 0.4
OUTLET_W = 4.0

LANES = 128
ROWS = 64
TILES = 32
WT = TILES + 4
WR = 80
BASE = 8
INNER = range(BASE + 4, BASE + ROWS - 8, 8)
BACK = range(INNER[0] + 8, INNER[-1], 8)
COLS = TILES * LANES
WCOLS = WT * LANES
MCOLS = WCOLS + 4 * LANES
F32 = jnp.float32
MIB = 1 << 20
FIRST_MIB = 27
STACK = 6
UNROLL = 8
PACK_BLOCKS = 4
PARTS = 4


def places():
    gx, gy = lax.axis_index("gx"), lax.axis_index("gy")
    return (
        gx, lax.axis_size("gx") - 1 - gx, gy, lax.axis_size("gy") - 1 - gy,
        lax.rem(gy, 2), lax.rem(gx, 2),
    )


VM = pl.BlockSpec(memory_space=pltpu.VMEM)
SM = pl.BlockSpec(memory_space=pltpu.SMEM)
HB = pl.BlockSpec(memory_space=pltpu.HBM)


def window(dtype=F32):
    return jax.ShapeDtypeStruct((WT, WR, LANES), dtype)


def lane_iota(rows):
    return lax.broadcasted_iota(jnp.int32, (rows, LANES), 1)


def pack_lines(src, out, held, arrived, sent):
    n = out.shape[0]
    loads, stores = [], []
    for i in range(n):
        low = i * COLS - 2 * LANES
        high = low + WCOLS
        a, b = max(low, 0), min(high, n * COLS)
        at = a - low
        pieces = [(a, b, at)]
        if low < 0:
            pieces.append((0, 2 * LANES, 0))
        if high > n * COLS:
            pieces.append((n * COLS - 2 * LANES, n * COLS, WCOLS - 2 * LANES))
        loads.append([
            pltpu.make_async_copy(
                src.at[0, :, a:b], held.at[i, :, at : at + b - a], arrived.at[i, k]
            )
            for k, (a, b, at) in enumerate(pieces)
        ])
        stores.append(pltpu.make_async_copy(held.at[i], out.at[i], sent.at[i]))
    for group in loads:
        for c in group:
            c.start()
    for group, store in zip(loads, stores):
        for c in group:
            c.wait()
        store.start()
    for store in stores:
        store.wait()


def all_fields(kd, v, s, c, t, at):
    kind = c[at]
    return (
        kd[at], *[v[(d, *at)] for d in range(3)],
        jnp.where(kind == 1, s[at], 0.0),
        jnp.where(kind == 2, DRAIN, 0.0).astype(F32),
        t[at],
    )


def pack_sides(kdl, kdr, vl, vr, sl, sr, cl, cr, tl, tr, side_a, side_b):
    odd = places()[5] == 1
    lo = lane_iota(ROWS) < NZ

    def layers(refs, near, far, low_side):
        def tile(k):
            return all_fields(*refs, (slice(None), slice(k * LANES, (k + 1) * LANES)))
        part = tile(far)
        merged = []
        for p in range(3):
            first, second = part[2 * p], part[2 * p + 1]
            if low_side:
                second = pltpu.roll(second, NZ, 1)
            else:
                first = pltpu.roll(first, NZ, 1)
            merged.append(jnp.where(lo, first, second))
        return list(tile(near)) + merged

    low_side = layers((kdl, vl, sl, cl, tl), 0, 1, True)
    high_side = layers((kdr, vr, sr, cr, tr), 1, 0, False)
    for f, (low, high) in enumerate(zip(low_side, high_side)):
        side_a[f] = jnp.where(odd, low, high)
        side_b[f] = jnp.where(odd, high, low)


def stack_fields(side, codes, code_rows, kd, s, c, kdt, kdb, vt, vb, st, sb, ct, cb, tt, tb,
                 stack, line_a, line_b, found, count):
    stack[0] = kd[...]
    stack[1] = jnp.where(c[...] == 1, s[...], 0.0)
    stack[2] = jnp.where(c[...] == 2, DRAIN, 0.0).astype(F32)

    @pl.when(pl.program_id(0) == 0)
    def _():
        odd = places()[4] == 1
        low_line = all_fields(kdt, vt, st, ct, tt, (slice(0, 2), slice(None)))
        high_line = all_fields(kdb, vb, sb, cb, tb, (slice(6, 8), slice(None)))
        for f, (low, high) in enumerate(zip(low_line, high_line)):
            line_a[f] = jnp.where(odd, low, high)
            line_b[f] = jnp.where(odd, high, low)


    @pl.when(pl.program_id(0) == 0)
    def _():
        count[0] = 0

    unroll = 32
    share = code_rows.shape[0] // PACK_BLOCKS
    for k in range(share):
        row = pl.program_id(0) * share + k

        @pl.when(jnp.max(code_rows[pl.ds(row, 1), :].astype(F32)) >= 0.0)
        def _():
            def compact(i, n):
                values = [codes[row * LANES + i * unroll + j] for j in range(unroll)]
                for value in values:
                    found[n] = value
                    n = n + 1 + (value >> 31)
                return n

            count[0] = lax.fori_loop(0, LANES // unroll, compact, count[0])


def coefficients(v0, v1, v2, drain):
    z = lax.broadcasted_iota(jnp.int32, v0.shape, v0.ndim - 1) & (NZ - 1)
    north = DISP - jnp.minimum(v0, 0.0)
    south = v0 + north
    east = DISP - jnp.minimum(v1, 0.0)
    west = v1 + east
    rise = DISP - jnp.minimum(v2, 0.0)
    up = jnp.where(z == NZ - 1, 0.0, rise)
    down = jnp.where(z == 0, 0.0, v2 + rise)
    centre = ((north + south) + (east + west)) + ((up + down) + drain)
    return north, south, east, west, up, down, centre


def east_of(u, t, right, a, rows):
    here = pl.ds(a, rows)
    lo = lane_iota(rows) < NZ
    return pltpu.roll(jnp.where(lo, u[right, here, :], u[t, here, :]), NZ, 1)


def flux(u, coef, src, t, right, a, rows, west):
    cn, cs, ce, cw, cu, cd, cc = coef
    here = pl.ds(a, rows)
    mid = u[t, here, :]
    north = u[t, pl.ds(a + 1, rows), :]
    south = u[t, pl.ds(a - 1, rows), :]
    east = east_of(u, t, right, a, rows)
    upper = pltpu.roll(mid, LANES - 1, 1)
    lower = pltpu.roll(mid, 1, 1)
    plane = cn[t, here, :] * north + cs[t, here, :] * south
    plane = plane + (ce[t, here, :] * east + cw[t, here, :] * west)
    plane = plane + (cu[t, here, :] * upper + cd[t, here, :] * lower)
    return mid, plane + (src[t, here, :] - cc[t, here, :] * mid), east


def flux_back(w, coef, t, left, right, a, rows):
    cn, cs, ce, cw, cu, cd, cc = coef
    here = pl.ds(a, rows)
    above, below = pl.ds(a + 1, rows), pl.ds(a - 1, rows)
    lo = lane_iota(rows) < NZ
    mid = w[t, here, :]
    w_right, w_left = w[right, here, :], w[left, here, :]
    from_low = cw[right, here, :] * w_right + ce[t, here, :] * mid
    from_high = cw[t, here, :] * mid + ce[left, here, :] * w_left
    total = pltpu.roll(jnp.where(lo, from_low, from_high), NZ, 1)
    total = total + (cs[t, above, :] * w[t, above, :] + cn[t, below, :] * w[t, below, :])
    total = total + pltpu.roll(cd[t, here, :] * mid, LANES - 1, 1)
    total = total + pltpu.roll(cu[t, here, :] * mid, 1, 1)
    return total - cc[t, here, :] * mid


def sorb(u):
    return jnp.exp((FREUND - 1.0) * jnp.log(u))


def rate_of(kd, power):
    return STEP / (1.0 + BULK * kd * power)


def first_half(lines, x_a, x_b, v_h, stack_h,
               u0, fst, d1, rate, power, cn, cs, ce, cw, cu, cd, cc, src, msg_a, msg_b,
               v, stack, sems):
    loads = []
    for k in range(PARTS):
        cols = pl.ds(k * COLS // PARTS, COLS // PARTS)
        loads.append([
            pltpu.make_async_copy(stack_h.at[0:3, :, cols], stack.at[:, :, cols], sems.at[2 * k]),
            pltpu.make_async_copy(v_h.at[:, :, cols], v.at[:, :, cols], sems.at[2 * k + 1]),
        ])
    for pair in loads:
        for load in pair:
            load.start()
    coef = (cn, cs, ce, cw, cu, cd, cc)
    own = pl.ds(BASE, ROWS)
    lines_of = lines.shape[1]
    for k in range(lines.shape[0]):
        for t in range(WT):
            u0[t, BASE + lines_of * k : BASE + lines_of * (k + 1), :] = lines[
                k, :, t * LANES : (t + 1) * LANES
            ]
    lo = lane_iota(ROWS) < NZ

    place = places()
    odd_x = place[5] == 1

    def both(f, rows=slice(None)):
        one, two = x_a[f, rows], x_b[f, rows]
        return jnp.where(odd_x, one, two), jnp.where(odd_x, two, one)

    low_x, high_x = zip(*[both(f) for f in range(6)])
    low_3, high_3 = zip(*[both(f) for f in range(7, 10)])

    def third(parts, f, high):
        part = parts[f // 2]
        if high:
            return jnp.where(lo, 0.0, part if f % 2 else pltpu.roll(part, NZ, 1))
        return jnp.where(lo, pltpu.roll(part, NZ, 1) if f % 2 else part, 0.0)

    for tile, fields in (
        (0, [third(low_3, f, True) for f in range(6)]),
        (1, low_x),
        (WT - 2, high_x),
        (WT - 1, [third(high_3, f, False) for f in range(6)]),
    ):
        for ref, val in zip(coef, coefficients(*fields[1:4], fields[5])):
            ref[tile, own, :] = val
        src[tile, own, :] = fields[4]
        rate[tile, own, :] = rate_of(fields[0], sorb(u0[tile, own, :]))

    @pl.when(place[0] == 0)
    def _():
        for ref in (u0, rate):
            ref[0:2, own, :] = jnp.zeros((2, ROWS, LANES), F32)

    @pl.when(place[1] == 0)
    def _():
        for ref in (u0, rate):
            ref[WT - 2 : WT, own, :] = jnp.zeros((2, ROWS, LANES), F32)

    def prepare(t, carry):
        cols = pl.ds(pl.multiple_of(t * LANES, LANES), LANES)
        for r in range(0, ROWS, 8):
            rr, at = pl.ds(r, 8), pl.ds(BASE + r, 8)
            p = sorb(u0[t + 2, at, :])
            power[t, rr, :] = p
            rate[t + 2, at, :] = rate_of(stack[0, rr, cols], p)
            values = coefficients(
                v[0, rr, cols], v[1, rr, cols], v[2, rr, cols], stack[2, rr, cols]
            )
            for ref, val in zip(coef, values):
                ref[t + 2, at, :] = val
            src[t + 2, at, :] = stack[1, rr, cols]
        return carry

    for k, pair in enumerate(loads):
        for load in pair:
            load.wait()
        lax.fori_loop(k * TILES // PARTS, (k + 1) * TILES // PARTS, prepare, 0, unroll=UNROLL)

    spans = range(BASE, BASE + ROWS, 8)

    def step(t, wests):
        right = jnp.minimum(t + 1, WT - 1)
        easts = []
        for a, west in zip(spans, wests):
            at = pl.ds(a, 8)
            mid, f, east = flux(u0, coef, src, t, right, a, 8, west)
            d = rate[t, at, :] * f
            d1[t, at, :] = d
            fst[t, at, :] = mid + d
            easts.append(east)
        return tuple(easts)

    first_west = tuple(east_of(u0, 0, 0, a, 8) for a in spans)
    lax.fori_loop(0, WT, step, first_west, unroll=UNROLL)

    top = BASE + ROWS
    odd = place[4] == 1

    def send(at, row, up, low):
        msg_a[row, at] = jnp.where(odd, low, up)
        msg_b[row, at] = jnp.where(odd, up, low)

    for t in range(WT):
        at = pl.ds(t * LANES, LANES)
        send(at, slice(0, 2), u0[t, top - 2 : top, :], u0[t, BASE : BASE + 2, :])
        send(at, slice(2, 4), fst[t, top - 3 : top - 1, :], fst[t, BASE + 1 : BASE + 3, :])
    blank = jnp.zeros((1, LANES), F32)
    for k in range(16):
        at = pl.ds(WCOLS + (k % 4) * LANES, LANES)
        row = slice(k // 4, k // 4 + 1)
        if k < 14:
            up = both(k // 2, slice(ROWS - 1, ROWS))[k % 2]
            send(at, row, up, both(k // 2, slice(0, 1))[k % 2])
        else:
            send(at, row, blank, blank)


def second_step(fst, coef, src, rate, target, d2, mis, w, spans):
    def step(t, wests):
        easts = []
        for a, west in zip(spans, wests):
            at = pl.ds(a, 8)
            mid, f, east = flux(fst, coef, src, t, t + 1, a, 8, west)
            rt = rate[t, at, :]
            d = rt * f
            d2[t, at, :] = d
            m = (mid + d) - target[t, at, :]
            mis[t, at, :] = m
            w[t, at, :] = m * rt
            easts.append(east)
        return tuple(easts)

    return step, tuple(east_of(fst, 0, 1, a, 8) for a in spans)


def weigh_outlets(found, count, mis, w, inner):
    lane = lax.broadcasted_iota(jnp.int32, (1, LANES), 1)

    def weigh(i, carry):
        code = found[i]
        row, col = code >> 16, (code >> 6) & 127
        within = (row >= INNER[0]) & (row < INNER[-1] + 8)
        at = pl.ds(row, 1)
        tile = col >> 1

        @pl.when(within if inner else jnp.logical_not(within))
        def _():
            hit = lane == (col & 1) * NZ + (code & (NZ - 1))
            factor = jnp.where(hit, 1.0 + OUTLET_W, 1.0)
            mis[tile, at, :] = mis[tile, at, :] * factor
            w[tile, at, :] = w[tile, at, :] * factor

        return carry

    lax.fori_loop(0, count[0], weigh, 0)


def adjoint_step(coef, rate, mis, w, grad, w1, spans):
    def back(t, carry):
        for a in spans:
            at = pl.ds(a, 8)
            g = mis[t, at, :] + flux_back(w, coef, t, t - 1, t + 1, a, 8)
            grad[t, at, :] = g
            w1[t, at, :] = g * rate[t, at, :]
        return carry

    return back


def middle(found, count, x_a, x_b, y_a, y_b, t_h, fst, rate,
           cn_in, cs_in, ce_in, cw_in, cu_in, cd_in, cc_in, src_in,
           cn, cs, ce, cw, cu, cd, cc, src, target, kd_edge, d2, mis, w, grad, w1,
           tgt, halo, sem):
    load = pltpu.make_async_copy(t_h, tgt, sem)
    load.start()
    coef = (cn, cs, ce, cw, cu, cd, cc)
    place = places()
    odd = place[4] == 1
    own = pl.ds(BASE, ROWS)

    for parity, y_low, y_high in ((True, y_a, y_b), (False, y_b, y_a)):

        @pl.when(odd if parity else jnp.logical_not(odd))
        def _():
            for f in range(7):
                for t in range(TILES):
                    at = pl.ds(t * LANES, LANES)
                    halo[f, t, 6:8, :] = y_low[f, :, at]
                    halo[f, t, 8:10, :] = y_high[f, :, at]

    def edges(t, carry):
        for a, to in ((0, slice(0, BASE)), (8, slice(BASE + ROWS, WR))):
            at = pl.ds(a, 8)
            values = coefficients(*[halo[f, t, at, :] for f in (1, 2, 3, 5)])
            for ref, val in zip(coef, values):
                ref[t + 2, to, :] = val
            src[t + 2, to, :] = halo[4, t, at, :]
            target[t + 2, to, :] = halo[6, t, at, :]
            kd_edge[t + 2, at, :] = halo[0, t, at, :]
        return carry

    lax.fori_loop(0, TILES, edges, 0, unroll=4)
    load.wait()

    def targets(t, carry):
        at = pl.ds(pl.multiple_of(t * LANES, LANES), LANES)
        target[t + 2, own, :] = tgt[:, at]
        return carry

    lax.fori_loop(0, TILES, targets, 0, unroll=2)
    odd_x = place[5] == 1
    target[1, own, :] = jnp.where(odd_x, x_a[6], x_b[6])
    target[WT - 2, own, :] = jnp.where(odd_x, x_b[6], x_a[6])

    step, start = second_step(fst, coef, src, rate, target, d2, mis, w, INNER)
    lax.fori_loop(1, WT - 1, step, start, unroll=UNROLL)
    weigh_outlets(found, count, mis, w, True)
    back = adjoint_step(coef, rate, mis, w, grad, w1, BACK)
    lax.fori_loop(1, WT - 1, back, 0, unroll=UNROLL)


def second_half(found, count, msg_a, msg_b, kd_h, power, kd_edge_in,
                u0_in, fst_in, d1_in, rate_in, cn_in, cs_in, ce_in, cw_in, cu_in, cd_in, cc_in, src_in,
                 target_in, d2_in, mis_in, w_in, grad_in, w1_in,
                kd_out_h, start_out_h,
                u0, fst, d1, rate, cn, cs, ce, cw, cu, cd, cc, src, target, d2, mis, w, grad, w1,
                kd, kd_out, start_out, halo, sems):
    load = pltpu.make_async_copy(kd_h, kd, sems.at[0, 0])
    load.start()
    coef = (cn, cs, ce, cw, cu, cd, cc)
    low8, high8 = slice(0, BASE), slice(BASE + ROWS, WR)
    top = BASE + ROWS
    place = places()
    odd = place[4] == 1

    def arrived(row, at):
        one, two = msg_a[row, at], msg_b[row, at]
        return jnp.where(odd, one, two), jnp.where(odd, two, one)

    for t in range(WT):
        at = pl.ds(t * LANES, LANES)
        low, high = arrived(slice(0, 4), at)
        u0[t, 6:8, :] = low[0:2]
        fst[t, 5:7, :] = low[2:4]
        u0[t, top : top + 2, :] = high[0:2]
        fst[t, top + 1 : top + 3, :] = high[2:4]

    for f in range(7):
        for n in range(4):
            halo[f, n] = jnp.zeros((16, LANES), F32)
        for side, n in ((0, 1), (1, 2)):
            k = 2 * f + side
            low, high = arrived(slice(k // 4, k // 4 + 1), pl.ds(WCOLS + (k % 4) * LANES, LANES))
            halo[f, n, 7:8, :] = low
            halo[f, n, 8:9, :] = high
    for n, t in enumerate((0, 1, WT - 2, WT - 1)):
        for a, to in ((0, low8), (8, high8)):
            at = pl.ds(a, 8)
            values = coefficients(*[halo[f, n, at, :] for f in (1, 2, 3, 5)])
            for ref, val in zip(coef, values):
                ref[t, to, :] = val
            src[t, to, :] = halo[4, n, at, :]
            target[t, to, :] = halo[6, n, at, :]
            rate[t, to, :] = rate_of(halo[0, n, at, :], sorb(u0[t, to, :]))

    def edges(t, carry):
        for a, to in ((0, low8), (8, high8)):
            rate[t, to, :] = rate_of(kd_edge_in[t, pl.ds(a, 8), :], sorb(u0[t, to, :]))
        return carry

    lax.fori_loop(2, WT - 2, edges, 0, unroll=8)

    zero8 = jnp.zeros((WT, BASE, LANES), F32)
    edge_rows = (low8, high8)

    @pl.when(place[0] == 0)
    def _():
        for to in edge_rows:
            rate[0:2, to, :] = zero8[:2]
            u0[0:2, to, :] = zero8[:2]

    @pl.when(place[1] == 0)
    def _():
        for to in edge_rows:
            rate[WT - 2 : WT, to, :] = zero8[:2]
            u0[WT - 2 : WT, to, :] = zero8[:2]

    @pl.when(place[2] == 0)
    def _():
        rate[:, low8, :] = zero8
        u0[:, low8, :] = zero8
        fst[:, low8, :] = zero8

    @pl.when(place[3] == 0)
    def _():
        rate[:, high8, :] = zero8
        u0[:, high8, :] = zero8
        fst[:, high8, :] = zero8

    edge_spans = ((BASE - 4, BASE - 1), (top - 4, top - 1))

    def edge_step(t, wests):
        right = jnp.minimum(t + 1, WT - 1)
        easts = []
        for (a, r0), west in zip(edge_spans, wests):
            at = pl.ds(a, 8)
            row = lax.broadcasted_iota(jnp.int32, (8, LANES), 0) + a
            new = (row == r0) | (row == r0 + 1)
            mid, f, east = flux(u0, coef, src, t, right, a, 8, west)
            d = rate[t, at, :] * f
            d1[t, at, :] = jnp.where(new, d, d1[t, at, :])
            fst[t, at, :] = jnp.where(new, mid + d, fst[t, at, :])
            easts.append(east)
        return tuple(easts)

    first_west = tuple(east_of(u0, 0, 0, a, 8) for a, _ in edge_spans)
    lax.fori_loop(0, WT, edge_step, first_west, unroll=18)

    spans = range(BASE - 4, BASE + ROWS + 4, 8)
    outer = [a for a in spans if a not in INNER]
    step, start = second_step(fst, coef, src, rate, target, d2, mis, w, outer)
    lax.fori_loop(1, WT - 1, step, start, unroll=17)

    weigh_outlets(found, count, mis, w, False)
    back = adjoint_step(coef, rate, mis, w, grad, w1, [a for a in spans if a not in BACK])
    lax.fori_loop(1, WT - 1, back, 0, unroll=UNROLL)
    load.wait()

    def last(t, carry):
        cols = pl.ds(pl.multiple_of(t * LANES, LANES), LANES)
        tw = t + 2
        for r in range(0, ROWS, 8):
            a = BASE + r
            at, rr = pl.ds(a, 8), pl.ds(r, 8)
            g = grad[tw, at, :]
            start = g + flux_back(w1, coef, tw, tw - 1, tw + 1, a, 8)
            both = mis[tw, at, :] * d2[tw, at, :] + g * d1[tw, at, :]
            kdg = (both * rate[tw, at, :]) * (power[t, rr, :] * (-BULK / STEP))
            kd_out[rr, cols] = kdg
            start_out[rr, cols] = start + kdg * kd[rr, cols] * (FREUND - 1.0) / u0[tw, at, :]
        return carry

    parts = PARTS
    stores = []
    for k in range(parts):
        lax.fori_loop(k * TILES // parts, (k + 1) * TILES // parts, last, 0, unroll=UNROLL)
        cols = pl.ds(k * COLS // parts, COLS // parts)
        for a, b, n in ((kd_out, kd_out_h, 2), (start_out, start_out_h, 3)):
            stores.append(pltpu.make_async_copy(a.at[:, cols], b.at[:, cols], sems.at[n, k]))
            stores[-1].start()
    for store in stores:
        store.wait()


def params(mib):
    return pltpu.CompilerParams(vmem_limit_bytes=mib * MIB)


def swap(a, b, axis):
    n = lax.axis_size(axis)

    def pairs(first):
        return [(i, j) for k in range(first, n - 1, 2) for i, j in ((k, k + 1), (k + 1, k))]

    return lax.ppermute(a, axis, pairs(0)), lax.ppermute(b, axis, pairs(1))


def per_device(checkpoint, sorption_kd, velocity, source, target, cell_type, outlets):
    n_gx = lax.axis_size("gx")
    gx, gy = lax.axis_index("gx"), lax.axis_index("gy")
    lines = pl.pallas_call(
        pack_lines,
        out_shape=jax.ShapeDtypeStruct((n_gx, checkpoint.shape[1], WCOLS), F32),
        in_specs=[HB],
        out_specs=HB,
        scratch_shapes=[
            pltpu.VMEM((n_gx, checkpoint.shape[1], WCOLS), F32),
            pltpu.SemaphoreType.DMA((n_gx, 2)),
            pltpu.SemaphoreType.DMA((n_gx,)),
        ],
        compiler_params=params(60),
        name="pack_lines",
    )(checkpoint)
    arrived = lax.all_to_all(lines, "gx", split_axis=0, concat_axis=0, tiled=True)

    side = jax.ShapeDtypeStruct((10, ROWS, LANES), F32)
    line = jax.ShapeDtypeStruct((7, 2, COLS), F32)
    row = (outlets >> 16) - gy * ROWS + BASE
    col = ((outlets >> 6) & 1023) - gx * (COLS // NZ) + 4
    inside = (row >= BASE - 2) & (row < BASE + ROWS + 2) & (col >= 2) & (col < 70)
    codes = jnp.where(inside, (row << 16) + (col << 6) + (outlets & (NZ - 1)), -1)
    code_rows = codes.reshape(-1, LANES)
    rows = ROWS // PACK_BLOCKS
    flat = pl.BlockSpec((rows, COLS), lambda i: (i, 0))
    two = 2 * LANES

    def block_specs(lead, *blocks):
        return [
            pl.BlockSpec(lead + shape, lambda i, at=at: (0,) * len(lead) + at) for shape, at in blocks
        ]

    sides = ((ROWS, two), (0, 0)), ((ROWS, two), (0, TILES // 2 - 1))
    ends = ((8, COLS), (0, 0)), ((8, COLS), (ROWS // 8 - 1, 0))
    fields = (sorption_kd, velocity, source, cell_type, target)
    twice = [f for f in fields for _ in range(2)]

    def specs(blocks):
        return [b for f in fields for b in block_specs((3,) if f.ndim == 3 else (), *blocks)]

    whole = lambda a: pl.BlockSpec(a.shape, lambda i: (0, 0, 0))
    side_a, side_b = pl.pallas_call(
        pack_sides,
        grid=(1,),
        out_shape=[side, side],
        in_specs=specs(sides),
        out_specs=[whole(side), whole(side)],
        compiler_params=params(60),
        name="pack_sides",
    )(*twice)
    stack, line_a, line_b, found, count = pl.pallas_call(
        stack_fields,
        grid=(PACK_BLOCKS,),
        out_shape=[
            jax.ShapeDtypeStruct((STACK, ROWS, COLS), F32), line, line,
            jax.ShapeDtypeStruct((outlets.shape[0],), jnp.int32),
            jax.ShapeDtypeStruct((1,), jnp.int32),
        ],
        in_specs=[HB, SM, pl.BlockSpec(code_rows.shape, lambda i: (0, 0)), flat, flat, flat]
        + specs(ends),
        out_specs=[
            pl.BlockSpec((3, rows, COLS), lambda i: (0, i, 0)), whole(line), whole(line), SM, SM,
        ],
        compiler_params=params(60),
        name="stack_fields",
    )(side_a, codes, code_rows, sorption_kd, source, cell_type, *twice)
    x_a, x_b = swap(side_a, side_b, "gx")
    y_a, y_b = swap(line_a, line_b, "gy")

    message = jax.ShapeDtypeStruct((4, MCOLS), F32)
    power = jax.ShapeDtypeStruct((TILES, ROWS, LANES), F32)
    u0, fst, d1, rate, power, *rest = pl.pallas_call(
        first_half,
        out_shape=[window()] * 4 + [power] + [window()] * 8 + [message] * 2,
        in_specs=[VM] * 3 + [HB] * 2,
        out_specs=[VM] * 15,
        scratch_shapes=[*[pltpu.VMEM((3, ROWS, COLS), F32)] * 2, pltpu.SemaphoreType.DMA((2 * PARTS,))],
        compiler_params=params(FIRST_MIB),
        name="first_half",
    )(arrived, x_a, x_b, velocity, stack)
    coefs, (msg_a, msg_b) = rest[:8], rest[8:]
    got_a, got_b = swap(msg_a, msg_b, "gy")

    edge_kd = jax.ShapeDtypeStruct((WT, 16, LANES), F32)
    *coefs, aim, kd_edge, d2, mis, w, grad, w1 = pl.pallas_call(
        middle,
        out_shape=[window()] * 9 + [edge_kd] + [window()] * 5,
        in_specs=[SM] * 2 + [VM] * 4 + [HB] + [VM] * 10,
        out_specs=[VM] * 15,
        input_output_aliases={9 + k: k for k in range(8)},
        scratch_shapes=[
            pltpu.VMEM((ROWS, COLS), F32),
            pltpu.VMEM((7, TILES, 16, LANES), F32),
            pltpu.SemaphoreType.DMA,
        ],
        compiler_params=params(8),
        name="middle",
    )(found, count, x_a, x_b, y_a, y_b, target, fst, rate, *coefs)

    kept = (u0, fst, d1, rate, *coefs, aim, d2, mis, w, grad, w1)
    plane = jax.ShapeDtypeStruct((ROWS, COLS), F32)
    outs = pl.pallas_call(
        second_half,
        out_shape=[plane, plane] + [window()] * 18,
        in_specs=[SM] * 2 + [VM] * 2 + [HB] + [VM] * 20,
        out_specs=[HB] * 2 + [VM] * 18,
        input_output_aliases={7 + k: 2 + k for k in range(18)},
        scratch_shapes=[
            *[pltpu.VMEM((ROWS, COLS), F32)] * 3,
            pltpu.VMEM((7, 4, 16, LANES), F32),
            pltpu.SemaphoreType.DMA((4, 4)),
        ],
        compiler_params=params(12),
        name="second_half",
    )(found, count, got_a, got_b, sorption_kd, power, kd_edge, *kept)
    return outs[0], outs[1]


def solution(mesh):
    return jax.shard_map(
        per_device,
        mesh=mesh,
        in_specs=(
            P("gy", "gx", None),
            P("gy", "gx"),
            P(None, "gy", "gx"),
            P("gy", "gx"),
            P("gy", "gx"),
            P("gy", "gx"),
            P(),
        ),
        out_specs=(P("gy", "gx"), P("gy", "gx")),
        check_vma=False,
    )
```
